512 devices in a mesh: gy: 16 (over y, core), gz: 32 (over x, z).
Axes of the slice: x: 4, y: 8, z: 8, core: 2. Of those that a mesh axis runs over, the one named last changes fastest.
Arguments:
- electric_level: float32 [256, 256, 128], P('gz', 'gy'), may hold values from -3 to 3
- impurity_atoms: int32 [256, 256, 128], P('gz', 'gy'), may hold values from 0 to 11
- cell_materials: int32 [256, 256, 128], P('gz', 'gy'), may hold values from 0 to 2, as said below
Outputs:
- updated: float32 [256, 256, 128], P('gz', 'gy')
The draws below stay inside these ranges and needn't reach their ends.
Inputs may be any that keep to these rules, and one draw needn't show every extreme that they name: `cell_materials`: material ids; the cells of one z line that are not silicon (0) all hold one material.
All inputs are finite; a program needn't handle non-finite values.
Results may differ from the reference program's by a relative error of at most 0.0015.
Values sent between devices are 32-bit elements; how exact they have to be, the bound alone decides.
A program may use at most 64 MiB of HBM per device.

```python
import jax
import jax.numpy as jnp
from jax import lax

NX = 128
ZW = 8192
NY = 256
NZ = 256


def draw_electric_level(key, part):
    rough_key = jax.random.fold_in(key, 11)
    values = jnp.clip(0.4 + 0.6 * jax.random.normal(rough_key, (NZ, NY, NX), jnp.float32), -3.0, 3.0)
    return values.astype(jnp.float32)


def draw_cell_materials(key, part):
    key = jax.random.fold_in(key, 21)
    column_kind = 1 + jax.random.randint(jax.random.fold_in(key, 1), (1, NY, NX), 0, 2)
    sprinkle = jax.random.randint(jax.random.fold_in(key, 2), (NZ, NY, NX), 0, 3)
    return jnp.where(sprinkle == 0, 0, column_kind).astype(jnp.int32)


def plant(entries, key, smallest, high):
    longest = entries.shape.index(max(entries.shape))
    spots = []
    for shift in (0, 1):
        where = [jax.random.randint(jax.random.fold_in(key, axis), (), 0, length) for axis, length in enumerate(entries.shape)]
        where[longest] = (where[longest] + shift) % entries.shape[longest]
        spots.append(tuple(where))
    return entries.at[spots[0]].set(smallest).at[spots[1]].set(high)


def setup_inputs(seed: int = 0) -> dict:
    key_list = jax.random.split(jax.random.key(seed), 4)
    return {
        "electric_level": draw_electric_level(jax.random.fold_in(key_list[3], 71), 0),
        "impurity_atoms": plant(jax.random.randint(key_list[1], (NZ, NY, NX), 0, 12), jax.random.fold_in(key_list[1], 1), 0, 11).astype(jnp.int32),
        "cell_materials": draw_cell_materials(jax.random.fold_in(key_list[3], 71), 0),
    }


def harmonic(own, other):
    other_fill = jnp.where(other > 0, other, own)
    return 2.0 * own * other_fill / (own + other_fill)

def beside_all(field):
    padded = jnp.pad(field, 1)
    return (padded[:-2, 1:-1, 1:-1], padded[2:, 1:-1, 1:-1], padded[1:-1, :-2, 1:-1], padded[1:-1, 2:, 1:-1], padded[1:-1, 1:-1, :-2], padded[1:-1, 1:-1, 2:])

def line_solve(lower, principal_entries, upper, rhs):
    sub_diag = jnp.moveaxis(lower, 0, -1)
    main_diag = jnp.moveaxis(principal_entries, 0, -1)
    upper_diagonal = jnp.moveaxis(upper, 0, -1)
    right = jnp.moveaxis(rhs, 0, -1)[..., None]
    solved_lines = lax.linalg.tridiagonal_solve(sub_diag, main_diag, upper_diagonal, right)[..., 0]
    return jnp.moveaxis(solved_lines, -1, 0)

def block_sum(field):
    depth, rows, cols = field.shape
    return field.reshape(depth, rows // 2, 2, cols // 2, 2).sum(axis=(2, 4))

def reference(electric_level, impurity_atoms, cell_materials):
    z_weight = ZW * 1.0
    permit = jnp.where(cell_materials == 0, 1.0, jnp.where(cell_materials == 1, 0.33, 0.64)).astype(jnp.float32)
    electron_population = (cell_materials == 0).astype(jnp.float32)
    volume_ionic_excess = electron_population * (0.5 * impurity_atoms.astype(jnp.float32) - 1.5)
    near_perm = beside_all(permit)
    weights = (z_weight, z_weight, 1.0, 1.0, 1.0, 1.0)
    faces = [weight_val * harmonic(permit, other) for weight_val, other in zip(weights, near_perm)]
    neighbour_link_total = faces[0] + faces[1] + faces[2] + faces[3] + faces[4] + faces[5]
    near_pot = beside_all(electric_level)
    collected_entries = faces[0] * near_pot[0]
    for index in range(1, 6):
        collected_entries = collected_entries + faces[index] * near_pot[index]
    source_vector = neighbour_link_total * electric_level - collected_entries + electron_population * 2.0 * jnp.sinh(electric_level) - volume_ionic_excess
    rhs = -source_vector
    principal_entries = neighbour_link_total + electron_population * 2.0 * jnp.cosh(electric_level)
    lower = jnp.where(near_perm[0] > 0, -faces[0], 0.0)
    upper = jnp.where(near_perm[1] > 0, -faces[1], 0.0)
    colour = ((jnp.arange(NY)[:, None] + jnp.arange(NX)[None, :]) % 2)[None]
    first = jnp.where(colour == 0, line_solve(lower, principal_entries, upper, rhs), 0.0)
    near_first = beside_all(first)
    side = faces[2] * near_first[2] + faces[3] * near_first[3] + faces[4] * near_first[4] + faces[5] * near_first[5]
    delta = first + jnp.where(colour == 1, line_solve(lower, principal_entries, upper, rhs + side), 0.0)
    near_delta = beside_all(delta)
    applied = principal_entries * delta
    for index in range(6):
        applied = applied - faces[index] * near_delta[index]
    resid = rhs - applied
    x_inner = faces[5][:, :, 0::2].reshape(NZ, NY // 2, 2, NX // 2).sum(axis=2)
    y_inner = faces[3][:, 0::2, :].reshape(NZ, NY // 2, NX // 2, 2).sum(axis=3)
    coarse_diag = block_sum(principal_entries) - 2.0 * (x_inner + y_inner)
    coarse = line_solve(block_sum(lower), coarse_diag, block_sum(upper), block_sum(resid))
    spread = jnp.repeat(jnp.repeat(coarse, 2, axis=1), 2, axis=2)
    return electric_level + delta + spread
```

```python
import jax
import jax.numpy as jnp
from jax import lax
from jax.experimental import pallas as pl
from jax.experimental.pallas import tpu as pltpu
from jax.sharding import PartitionSpec as P

MESH = pl.DeviceIdType.MESH
ZW = 8192.0
SEGS = 32
GYS = 16
F32 = jnp.float32


def hops(k):
    x, z = k // 8, k % 8
    return min(x, 4 - x) + min(z, 8 - z)


ORDER = sorted(
    ((k, h) for k in range(16) for h in (0, 1)), key=lambda kh: -hops((2 * kh[0] + kh[1]) % 32)
)


def roll_l(v, s):
    return pltpu.roll(v, s % 128, 1)


def roll_r(v, s):
    return pltpu.roll(v, s % 16, 0)


def swap_blocks(rows, blk):
    rows = list(rows)
    for bit in (1, 2, 4):
        keep = (blk & bit) == 0
        for i in range(8):
            if not i & bit:
                a, c = rows[i], rows[i | bit]
                rows[i] = jnp.where(keep, a, roll_l(c, 16 * bit))
                rows[i | bit] = jnp.where(keep, roll_l(a, -16 * bit), c)
    return rows


def face(a, b):
    total = a + b
    prod = a * b
    return jnp.where(prod > 0, 2.0 * prod / total, total)


def own_rows(half):
    return ((0, 4, 11), (5, 1, 11))[half]


def edge_rows(half):
    return ((13, 1, 3), (0, 12, 3))[half]


def eliminate(cond, excess, first_link, inv_ref, m_ref, h_ref, blk):
    zero = jnp.zeros_like(first_link)

    def step(i, carry):
        link_a, in_a, g_l, link_b, in_b, g_r = carry
        j = 30 - i
        g = excess[i] + in_a
        k = cond[i]
        inv = 1.0 / (link_a + k + g)
        m = k * inv
        h = link_a * inv
        inv_ref[i] = inv
        m_ref[i] = m
        h_ref[i] = h
        gb = excess[j] + in_b
        kb = cond[j - 1]
        invb = 1.0 / (link_b + kb + gb)
        mb = kb * invb
        hb = link_b * invb
        inv_ref[j] = invb
        m_ref[j] = mb
        h_ref[j] = hb
        return (link_a * m, g * m, g_l + g * h, link_b * mb, gb * mb, g_r + gb * hb)

    link_a, in_a, g_l, link_b, in_b, g_r = lax.fori_loop(
        0, 15, step, (first_link, zero, zero, cond[30], zero, zero), unroll=True
    )
    g = excess[15] + in_a + in_b
    inv = 1.0 / (link_a + link_b + g)
    ha = link_a * inv
    hb = link_b * inv
    inv_ref[15] = inv
    h_ref[15] = ha
    m_ref[15] = hb
    low = link_a * hb
    g_l = g_l + ha * g
    g_r = g_r + hb * g
    ground = excess[31] + g_r + roll_l(g_l, -16)
    up = roll_l(low, -16)
    factors = []
    for s in (16, 32, 64):
        inv = 1.0 / (low + up + ground)
        alpha = low * roll_l(inv, s)
        beta = up * roll_l(inv, -s)
        ground, low, up = (
            ground + alpha * roll_l(ground, s) + beta * roll_l(ground, -s),
            alpha * roll_l(low, s),
            beta * roll_l(up, -s),
        )
        factors.append((s, alpha, beta))
    return factors, 1.0 / ground


def line_solve(rhs, factors, inv_ref, m_ref, h_ref, b_ref, x_ref):
    seps, inv_sep = factors
    zero = jnp.zeros_like(inv_sep)

    def forward(i, carry):
        in_a, b_l, in_b, b_r = carry
        j = 30 - i
        b = rhs[i] + in_a
        bb = rhs[j] + in_b
        b_ref[i] = b
        b_ref[j] = bb
        return (m_ref[i] * b, b_l + h_ref[i] * b, m_ref[j] * bb, b_r + h_ref[j] * bb)

    in_a, b_l, in_b, b_r = lax.fori_loop(0, 15, forward, (zero, zero, zero, zero), unroll=True)
    mid = rhs[15] + in_a + in_b
    b_l = b_l + h_ref[15] * mid
    b_r = b_r + m_ref[15] * mid
    b = rhs[31] + b_r + roll_l(b_l, -16)
    for s, alpha, beta in seps:
        b = b + alpha * roll_l(b, s) + beta * roll_l(b, -s)
    x_r = b * inv_sep
    x_l = roll_l(x_r, 16)
    x_ref[31] = x_r
    mid = inv_ref[15] * mid + h_ref[15] * x_l + m_ref[15] * x_r
    x_ref[15] = mid

    def backward(n, carry):
        x_a, x_b = carry
        i = 14 - n
        j = 16 + n
        x_a = m_ref[i] * x_a + (inv_ref[i] * b_ref[i] + h_ref[i] * x_l)
        x_b = m_ref[j] * x_b + (inv_ref[j] * b_ref[j] + h_ref[j] * x_r)
        x_ref[i] = x_a
        x_ref[j] = x_b
        return (x_a, x_b)

    lax.fori_loop(0, 15, backward, (mid, mid), unroll=True)


def kernel(
    v_ref, imp_ref, mat_ref, o_ref,
    pack, recv, send_back, got_back, grid, cond, excess, rhs0, rhs1, fx, fy, ccond, cexcess,
    inv, m, h, cinv, cm, ch, bb, x0, x1, xc,
    send_sem, recv_sem, edge_send, edge_recv, back_send, back_recv,
):
    gy, gz = lax.axis_index("gy"), lax.axis_index("gz")
    half, tile = lax.rem(gz, 2), gz // 2
    above = lax.rem(gy + GYS - 1, GYS)
    below = lax.rem(gy + 1, GYS)
    mine_edge = lax.rem(gy + GYS - 1 + 2 * half, GYS)

    barrier = pltpu.get_barrier_semaphore()
    for k in sorted(range(SEGS), key=lambda k: -hops(k)):
        other = lax.rem(gz + k, SEGS)
        if k:
            pl.semaphore_signal(barrier, 1, device_id=(gy, other), device_id_type=MESH)
        pl.semaphore_signal(barrier, 1, device_id=(mine_edge, other), device_id_type=MESH)

    lane = lax.broadcasted_iota(jnp.int32, (16, 128), 1)
    row = lax.broadcasted_iota(jnp.int32, (16, 128), 0)
    blk = lane // 16
    win = lax.rem(lane, 16)

    for a in range(3):
        for odd in (0, 1):
            planes = []
            for z in range(8):
                v = v_ref[z]
                mat = mat_ref[z]
                if a == 0:
                    f = v
                elif a == 1:
                    f = jnp.where(mat == 0, 1.0, jnp.where(mat == 1, 0.33, 0.64)).astype(F32)
                else:
                    charge = 0.5 * imp_ref[z].astype(F32) - 1.5
                    f = jnp.where(mat == 0, jnp.exp(v) - jnp.exp(-v) - charge, 0.0)
                planes.append(roll_l(f, -4 if odd else 4))
            for t, f in enumerate(swap_blocks(planes, blk)):
                pack[2 * t + odd, a] = f

    pl.semaphore_wait(barrier, SEGS - 1 + SEGS)

    def own_copy(to, hf):
        s, d, n = own_rows(hf)
        return pltpu.make_async_remote_copy(
            src_ref=pack.at[to // 2, :, pl.ds(s, n)],
            dst_ref=recv.at[gz, :, pl.ds(d, n)],
            send_sem=send_sem.at[to],
            recv_sem=recv_sem.at[gz],
            device_id=(gy, to),
            device_id_type=MESH,
        )

    def edge_copy(to, hf):
        s, d, n = edge_rows(hf)
        return pltpu.make_async_remote_copy(
            src_ref=pack.at[to // 2, :, pl.ds(s, n)],
            dst_ref=recv.at[gz, :, pl.ds(d, n)],
            send_sem=edge_send.at[to],
            recv_sem=edge_recv.at[gz],
            device_id=(below if hf == 0 else above, to),
            device_id_type=MESH,
        )

    for k, hf in ORDER:
        to = 2 * lax.rem(tile + k, 16) + hf
        if k:
            own_copy(to, hf).start()
        else:

            @pl.when(half == hf)
            def _():
                s, d, n = own_rows(hf)
                pltpu.make_async_copy(
                    pack.at[to // 2, :, pl.ds(s, n)], recv.at[gz, :, pl.ds(d, n)], recv_sem.at[gz]
                ).start()

            @pl.when(half != hf)
            def _():
                own_copy(to, hf).start()

        edge_copy(to, hf).start()

    y = gy * 16 + half * 8 - 4 + row
    x = tile * 8 - 4 + win
    inside = (row >= 1) & (row <= 14) & (y >= 0) & (y < GYS * 16) & (x >= 0) & (x < 128)
    odd_cell = lax.rem(row + win, 2) == 1
    colour0 = inside & jnp.logical_not(odd_cell)
    colour1 = inside & odd_cell

    def landed(s):
        pltpu.make_async_copy(
            recv.at[0, :, pl.ds(1, 11)], recv.at[0, :, pl.ds(1, 11)], recv_sem.at[s]
        ).wait()
        pltpu.make_async_copy(
            recv.at[0, :, pl.ds(1, 3)], recv.at[0, :, pl.ds(1, 3)], edge_recv.at[s]
        ).wait()

    def take(q, carry):
        for c in range(8):
            landed(4 * c + q)
        for a in range(3):
            parts = swap_blocks([recv[4 * c + q, a] for c in range(8)], blk)
            for z in range(8):
                grid[a, 8 * q + z] = jnp.where(inside, parts[z], 0.0)
        return carry

    lax.fori_loop(0, 4, take, 0)

    for a in range(2):
        grid[a, 32] = jnp.where(blk == 7, 0.0, roll_l(grid[a, 0], -16))

    k_last = ZW * face(grid[1, 31], grid[1, 32])
    flow_last = k_last * (grid[0, 32] - grid[0, 31])
    k_floor = ZW * grid[1, 0]
    at_floor = blk == 0
    first_link = jnp.where(at_floor, 0.0, roll_l(k_last, 16))
    flow_first = jnp.where(at_floor, k_floor * grid[0, 0], roll_l(flow_last, 16))
    outside_one = jnp.where(inside, 0.0, 1.0)

    def assemble(i, flow_below):
        v = grid[0, i]
        p = grid[1, i]
        kz = ZW * face(p, grid[1, i + 1])
        flow = kz * (grid[0, i + 1] - v)
        px = face(p, roll_l(p, -1))
        py = face(p, roll_r(p, -1))
        flow_x = px * (roll_l(v, -1) - v)
        flow_y = py * (roll_r(v, -1) - v)
        soft = jnp.where(p == 1.0, jnp.exp(v) + jnp.exp(-v), 0.0) + outside_one
        extra = (px + roll_l(px, 1)) + (py + roll_r(py, 1)) + soft
        force = (
            (flow - flow_below) + (flow_x - roll_l(flow_x, 1)) + (flow_y - roll_r(flow_y, 1)) - grid[2, i]
        )
        cond[i] = kz
        excess[i] = extra
        fx[i] = px
        fy[i] = py
        rhs0[i] = jnp.where(colour0, force, 0.0)
        rhs1[i] = jnp.where(colour1, force, 0.0)
        k2 = kz + roll_l(kz, -1)
        ccond[i] = k2 + roll_r(k2, -1)
        e2 = extra + roll_l(extra, -1) - 2.0 * px
        y2 = py + roll_l(py, -1)
        cexcess[i] = e2 + roll_r(e2, -1) - 2.0 * y2
        return flow

    lax.fori_loop(0, 32, assemble, flow_first)

    def quad(f):
        f = f + roll_l(f, -1)
        return f + roll_r(f, -1)

    floor = jnp.where(at_floor, k_floor, 0.0)
    roof = jnp.where(blk == 7, k_last, 0.0)
    excess[0] = excess[0] + floor
    excess[31] = excess[31] + roof
    cexcess[0] = cexcess[0] + quad(floor)
    cexcess[31] = cexcess[31] + quad(roof)

    fine = eliminate(cond, excess, first_link, inv, m, h, blk)
    coarse = eliminate(ccond, cexcess, quad(first_link), cinv, cm, ch, blk)

    line_solve(rhs0, fine, inv, m, h, bb, x0)

    def lateral(f, i):
        gx, gyy = fx[i], fy[i]
        return (gx * roll_l(f, -1) + roll_l(gx * f, 1)) + (gyy * roll_r(f, -1) + roll_r(gyy * f, 1))

    def side(i, carry):
        rhs1[i] = jnp.where(colour1, rhs1[i] + lateral(x0[i], i), 0.0)
        return carry

    lax.fori_loop(0, 32, side, 0)
    line_solve(rhs1, fine, inv, m, h, bb, x1)

    def restrict(i, carry):
        rhs0[i] = quad(jnp.where(colour0, lateral(x1[i], i), 0.0))
        return carry

    lax.fori_loop(0, 32, restrict, 0)
    line_solve(rhs0, coarse, cinv, cm, ch, bb, xc)

    even_x = lax.rem(lane, 2) == 0
    even_y = lax.rem(row, 2) == 0

    def give(q, carry):
        parts = []
        for z in range(8):
            i = 8 * q + z
            f = xc[i]
            f = jnp.where(even_x, f, roll_l(f, 1))
            f = jnp.where(even_y, f, roll_r(f, 1))
            parts.append((x0[i] + x1[i] + f)[4:12])
        for c, f in enumerate(swap_blocks(parts, blk[:8])):
            send_back[4 * c + q] = f
        return carry

    lax.fori_loop(0, 4, give, 0)

    def back_copy(to):
        return pltpu.make_async_remote_copy(
            src_ref=send_back.at[to],
            dst_ref=got_back.at[gz],
            send_sem=back_send.at[to],
            recv_sem=back_recv.at[gz],
            device_id=(gy, to),
            device_id_type=MESH,
        )

    for k in sorted(range(SEGS), key=lambda k: -hops(k)):
        to = lax.rem(gz + k, SEGS)
        if k:
            back_copy(to).start()
    got_back[gz] = send_back[gz]

    for k, hf in ORDER:
        to = 2 * lax.rem(tile + k, 16) + hf
        if k:
            own_copy(to, hf).wait_send()
        else:

            @pl.when(half != hf)
            def _():
                own_copy(to, hf).wait_send()

        edge_copy(to, hf).wait_send()

    for k in range(1, SEGS):
        s = lax.rem(gz + k, SEGS)
        pltpu.make_async_copy(send_back.at[0], send_back.at[0], back_recv.at[s]).wait()

    low8 = win[:8] < 8
    for hf in (0, 1):
        parts = []
        for t in range(8):
            e = got_back[4 * t + hf]
            o = got_back[4 * t + 2 + hf]
            parts.append(jnp.where(low8, roll_l(e, -4), roll_l(o, 4)))
        for z, f in enumerate(swap_blocks(parts, blk[:8])):
            o_ref[z, pl.ds(8 * hf, 8)] = v_ref[z, pl.ds(8 * hf, 8)] + f

    for k in range(1, SEGS):
        s = lax.rem(gz + k, SEGS)
        pltpu.make_async_copy(send_back.at[0], send_back.at[0], back_send.at[s]).wait()


def body(electric_level, impurity_atoms, cell_materials):
    line = pltpu.VMEM((32, 16, 128), F32)
    vmem = pl.BlockSpec(memory_space=pltpu.VMEM)
    return pl.pallas_call(
        kernel,
        out_shape=jax.ShapeDtypeStruct(electric_level.shape, F32),
        in_specs=[vmem] * 3,
        out_specs=vmem,
        scratch_shapes=[
            pltpu.VMEM((16, 3, 16, 128), F32),
            pltpu.VMEM((SEGS, 3, 16, 128), F32),
            pltpu.VMEM((SEGS, 8, 128), F32),
            pltpu.VMEM((SEGS, 8, 128), F32),
            pltpu.VMEM((3, 33, 16, 128), F32),
        ]
        + [line] * 18
        + [pltpu.SemaphoreType.DMA((SEGS,))] * 6,
        compiler_params=pltpu.CompilerParams(
            collective_id=0, has_side_effects=True, vmem_limit_bytes=32 * 1024 * 1024
        ),
        cost_estimate=pl.CostEstimate(flops=20_000_000, bytes_accessed=262144, transcendentals=200_000),
        name="newton_step",
    )(electric_level, impurity_atoms, cell_materials)


def solution(mesh):
    placed = P("gz", "gy", None)
    return jax.shard_map(
        body, mesh=mesh, in_specs=(placed,) * 3, out_specs=placed, check_vma=False
    )
```

```python
import jax
import jax.numpy as jnp
from jax import lax
from jax.experimental import pallas as pl
from jax.experimental.pallas import tpu as pltpu
from jax.sharding import PartitionSpec as P

MESH = pl.DeviceIdType.MESH
ZW = 8192.0
SEGS = 32
GYS = 16
F32 = jnp.float32


def hops(k):
    x, z = k // 8, k % 8
    return min(x, 4 - x) + min(z, 8 - z)


ORDER = sorted(
    ((k, h) for k in range(16) for h in (0, 1)), key=lambda kh: -hops((2 * kh[0] + kh[1]) % 32)
)


def roll_l(v, s):
    return pltpu.roll(v, s % 128, 1)


def roll_r(v, s):
    return pltpu.roll(v, s % 16, 0)


def swap_blocks(rows, blk):
    rows = list(rows)
    for bit in (1, 2, 4):
        keep = (blk & bit) == 0
        for i in range(8):
            if not i & bit:
                a, c = rows[i], rows[i | bit]
                rows[i] = jnp.where(keep, a, roll_l(c, 16 * bit))
                rows[i | bit] = jnp.where(keep, roll_l(a, -16 * bit), c)
    return rows


def face(a, b):
    total = a + b
    prod = a * b
    return jnp.where(prod > 0, 2.0 * prod / total, total)


def own_rows(half):
    return ((0, 4, 11), (5, 1, 11))[half]


def edge_rows(half):
    return ((13, 1, 3), (0, 12, 3))[half]


def eliminate(cond, excess, first_link, inv_ref, m_ref, h_ref, blk):
    zero = jnp.zeros_like(first_link)

    def step(i, carry):
        link_a, in_a, g_l, link_b, in_b, g_r = carry
        j = 30 - i
        g = excess[i] + in_a
        k = cond[i]
        inv = 1.0 / (link_a + k + g)
        m = k * inv
        h = link_a * inv
        inv_ref[i] = inv
        m_ref[i] = m
        h_ref[i] = h
        gb = excess[j] + in_b
        kb = cond[j - 1]
        invb = 1.0 / (link_b + kb + gb)
        mb = kb * invb
        hb = link_b * invb
        inv_ref[j] = invb
        m_ref[j] = mb
        h_ref[j] = hb
        return (link_a * m, g * m, g_l + g * h, link_b * mb, gb * mb, g_r + gb * hb)

    link_a, in_a, g_l, link_b, in_b, g_r = lax.fori_loop(
        0, 15, step, (first_link, zero, zero, cond[30], zero, zero), unroll=True
    )
    g = excess[15] + in_a + in_b
    inv = 1.0 / (link_a + link_b + g)
    ha = link_a * inv
    hb = link_b * inv
    inv_ref[15] = inv
    h_ref[15] = ha
    m_ref[15] = hb
    low = link_a * hb
    g_l = g_l + ha * g
    g_r = g_r + hb * g
    ground = excess[31] + g_r + roll_l(g_l, -16)
    up = roll_l(low, -16)
    factors = []
    for s in (16, 32, 64):
        inv = 1.0 / (low + up + ground)
        alpha = low * roll_l(inv, s)
        beta = up * roll_l(inv, -s)
        ground, low, up = (
            ground + alpha * roll_l(ground, s) + beta * roll_l(ground, -s),
            alpha * roll_l(low, s),
            beta * roll_l(up, -s),
        )
        factors.append((s, alpha, beta))
    return factors, 1.0 / ground


def line_solve(rhs, factors, inv_ref, m_ref, h_ref, b_ref, x_ref):
    seps, inv_sep = factors
    zero = jnp.zeros_like(inv_sep)

    def forward(i, carry):
        in_a, b_l, in_b, b_r = carry
        j = 30 - i
        b = rhs[i] + in_a
        bb = rhs[j] + in_b
        b_ref[i] = b
        b_ref[j] = bb
        return (m_ref[i] * b, b_l + h_ref[i] * b, m_ref[j] * bb, b_r + h_ref[j] * bb)

    in_a, b_l, in_b, b_r = lax.fori_loop(0, 15, forward, (zero, zero, zero, zero), unroll=True)
    mid = rhs[15] + in_a + in_b
    b_l = b_l + h_ref[15] * mid
    b_r = b_r + m_ref[15] * mid
    b = rhs[31] + b_r + roll_l(b_l, -16)
    for s, alpha, beta in seps:
        b = b + alpha * roll_l(b, s) + beta * roll_l(b, -s)
    x_r = b * inv_sep
    x_l = roll_l(x_r, 16)
    x_ref[31] = x_r
    mid = inv_ref[15] * mid + h_ref[15] * x_l + m_ref[15] * x_r
    x_ref[15] = mid

    def backward(n, carry):
        x_a, x_b = carry
        i = 14 - n
        j = 16 + n
        x_a = m_ref[i] * x_a + (inv_ref[i] * b_ref[i] + h_ref[i] * x_l)
        x_b = m_ref[j] * x_b + (inv_ref[j] * b_ref[j] + h_ref[j] * x_r)
        x_ref[i] = x_a
        x_ref[j] = x_b
        return (x_a, x_b)

    lax.fori_loop(0, 15, backward, (mid, mid), unroll=True)


def kernel(
    v_hbm, imp_hbm, mat_hbm, o_ref,
    v_ref, imp_ref, mat_ref, in_sem, pack, recv, send_back, got_back, grid, cond, excess, rhs0, rhs1, fx, fy, ccond, cexcess,
    inv, m, h, cinv, cm, ch, bb, x0, x1, xc,
    send_sem, recv_sem, edge_send, edge_recv, back_send, back_recv,
):
    gy, gz = lax.axis_index("gy"), lax.axis_index("gz")
    half, tile = lax.rem(gz, 2), gz // 2
    above = lax.rem(gy + GYS - 1, GYS)
    below = lax.rem(gy + 1, GYS)
    mine_edge = lax.rem(gy + GYS - 1 + 2 * half, GYS)

    fetch = [
        pltpu.make_async_copy(v_hbm, v_ref, in_sem.at[0]),
        pltpu.make_async_copy(mat_hbm, mat_ref, in_sem.at[1]),
        pltpu.make_async_copy(imp_hbm, imp_ref, in_sem.at[2]),
    ]
    for copy in fetch:
        copy.start()
    barrier = pltpu.get_barrier_semaphore()
    for k in sorted(range(SEGS), key=lambda k: -hops(k)):
        other = lax.rem(gz + k, SEGS)
        if k:
            pl.semaphore_signal(barrier, 1, device_id=(gy, other), device_id_type=MESH)
        pl.semaphore_signal(barrier, 1, device_id=(mine_edge, other), device_id_type=MESH)

    lane = lax.broadcasted_iota(jnp.int32, (16, 128), 1)
    row = lax.broadcasted_iota(jnp.int32, (16, 128), 0)
    blk = lane // 16
    win = lax.rem(lane, 16)

    for copy in fetch:
        copy.wait()

    for a in range(3):
        for odd in (0, 1):
            planes = []
            for z in range(8):
                v = v_ref[z]
                mat = mat_ref[z]
                if a == 0:
                    f = v
                elif a == 1:
                    f = jnp.where(mat == 0, 1.0, jnp.where(mat == 1, 0.33, 0.64)).astype(F32)
                else:
                    charge = 0.5 * imp_ref[z].astype(F32) - 1.5
                    f = jnp.where(mat == 0, jnp.exp(v) - jnp.exp(-v) - charge, 0.0)
                planes.append(roll_l(f, -4 if odd else 4))
            for t, f in enumerate(swap_blocks(planes, blk)):
                pack[2 * t + odd, a] = f

    pl.semaphore_wait(barrier, SEGS - 1 + SEGS)

    def own_copy(to, hf):
        s, d, n = own_rows(hf)
        return pltpu.make_async_remote_copy(
            src_ref=pack.at[to // 2, :, pl.ds(s, n)],
            dst_ref=recv.at[gz, :, pl.ds(d, n)],
            send_sem=send_sem.at[to],
            recv_sem=recv_sem.at[gz],
            device_id=(gy, to),
            device_id_type=MESH,
        )

    def edge_copy(to, hf):
        s, d, n = edge_rows(hf)
        return pltpu.make_async_remote_copy(
            src_ref=pack.at[to // 2, :, pl.ds(s, n)],
            dst_ref=recv.at[gz, :, pl.ds(d, n)],
            send_sem=edge_send.at[to],
            recv_sem=edge_recv.at[gz],
            device_id=(below if hf == 0 else above, to),
            device_id_type=MESH,
        )

    for k, hf in ORDER:
        to = 2 * lax.rem(tile + k, 16) + hf
        if k:
            own_copy(to, hf).start()
        else:

            @pl.when(half == hf)
            def _():
                s, d, n = own_rows(hf)
                pltpu.make_async_copy(
                    pack.at[to // 2, :, pl.ds(s, n)], recv.at[gz, :, pl.ds(d, n)], recv_sem.at[gz]
                ).start()

            @pl.when(half != hf)
            def _():
                own_copy(to, hf).start()

        edge_copy(to, hf).start()

    y = gy * 16 + half * 8 - 4 + row
    x = tile * 8 - 4 + win
    inside = (row >= 1) & (row <= 14) & (y >= 0) & (y < GYS * 16) & (x >= 0) & (x < 128)
    odd_cell = lax.rem(row + win, 2) == 1
    colour0 = inside & jnp.logical_not(odd_cell)
    colour1 = inside & odd_cell

    def landed(s):
        pltpu.make_async_copy(
            recv.at[0, :, pl.ds(1, 11)], recv.at[0, :, pl.ds(1, 11)], recv_sem.at[s]
        ).wait()
        pltpu.make_async_copy(
            recv.at[0, :, pl.ds(1, 3)], recv.at[0, :, pl.ds(1, 3)], edge_recv.at[s]
        ).wait()

    def take(q, carry):
        for c in range(8):
            landed(4 * c + q)
        for a in range(3):
            parts = swap_blocks([recv[4 * c + q, a] for c in range(8)], blk)
            for z in range(8):
                grid[a, 8 * q + z] = jnp.where(inside, parts[z], 0.0)
        return carry

    lax.fori_loop(0, 4, take, 0, unroll=4)

    for a in range(2):
        grid[a, 32] = jnp.where(blk == 7, 0.0, roll_l(grid[a, 0], -16))

    k_last = ZW * face(grid[1, 31], grid[1, 32])
    flow_last = k_last * (grid[0, 32] - grid[0, 31])
    k_floor = ZW * grid[1, 0]
    at_floor = blk == 0
    first_link = jnp.where(at_floor, 0.0, roll_l(k_last, 16))
    flow_first = jnp.where(at_floor, k_floor * grid[0, 0], roll_l(flow_last, 16))
    outside_one = jnp.where(inside, 0.0, 1.0)

    def assemble(i, flow_below):
        v = grid[0, i]
        p = grid[1, i]
        kz = ZW * face(p, grid[1, i + 1])
        flow = kz * (grid[0, i + 1] - v)
        px = face(p, roll_l(p, -1))
        py = face(p, roll_r(p, -1))
        flow_x = px * (roll_l(v, -1) - v)
        flow_y = py * (roll_r(v, -1) - v)
        soft = jnp.where(p == 1.0, jnp.exp(v) + jnp.exp(-v), 0.0) + outside_one
        extra = (px + roll_l(px, 1)) + (py + roll_r(py, 1)) + soft
        force = (
            (flow - flow_below) + (flow_x - roll_l(flow_x, 1)) + (flow_y - roll_r(flow_y, 1)) - grid[2, i]
        )
        cond[i] = kz
        excess[i] = extra
        fx[i] = px
        fy[i] = py
        rhs0[i] = jnp.where(colour0, force, 0.0)
        rhs1[i] = jnp.where(colour1, force, 0.0)
        k2 = kz + roll_l(kz, -1)
        ccond[i] = k2 + roll_r(k2, -1)
        e2 = extra + roll_l(extra, -1) - 2.0 * px
        y2 = py + roll_l(py, -1)
        cexcess[i] = e2 + roll_r(e2, -1) - 2.0 * y2
        return flow

    lax.fori_loop(0, 32, assemble, flow_first, unroll=32)

    def quad(f):
        f = f + roll_l(f, -1)
        return f + roll_r(f, -1)

    floor = jnp.where(at_floor, k_floor, 0.0)
    roof = jnp.where(blk == 7, k_last, 0.0)
    excess[0] = excess[0] + floor
    excess[31] = excess[31] + roof
    cexcess[0] = cexcess[0] + quad(floor)
    cexcess[31] = cexcess[31] + quad(roof)

    fine = eliminate(cond, excess, first_link, inv, m, h, blk)
    coarse = eliminate(ccond, cexcess, quad(first_link), cinv, cm, ch, blk)

    line_solve(rhs0, fine, inv, m, h, bb, x0)

    def lateral(f, i):
        gx, gyy = fx[i], fy[i]
        return (gx * roll_l(f, -1) + roll_l(gx * f, 1)) + (gyy * roll_r(f, -1) + roll_r(gyy * f, 1))

    def side(i, carry):
        rhs1[i] = jnp.where(colour1, rhs1[i] + lateral(x0[i], i), 0.0)
        return carry

    lax.fori_loop(0, 32, side, 0, unroll=32)
    line_solve(rhs1, fine, inv, m, h, bb, x1)

    def restrict(i, carry):
        rhs0[i] = quad(jnp.where(colour0, lateral(x1[i], i), 0.0))
        return carry

    lax.fori_loop(0, 32, restrict, 0, unroll=32)
    line_solve(rhs0, coarse, cinv, cm, ch, bb, xc)

    even_x = lax.rem(lane, 2) == 0
    even_y = lax.rem(row, 2) == 0

    def give(q, carry):
        parts = []
        for z in range(8):
            i = 8 * q + z
            f = xc[i]
            f = jnp.where(even_x, f, roll_l(f, 1))
            f = jnp.where(even_y, f, roll_r(f, 1))
            parts.append((x0[i] + x1[i] + f)[4:12])
        for c, f in enumerate(swap_blocks(parts, blk[:8])):
            send_back[4 * c + q] = f
        return carry

    lax.fori_loop(0, 4, give, 0, unroll=4)

    def back_copy(to):
        return pltpu.make_async_remote_copy(
            src_ref=send_back.at[to],
            dst_ref=got_back.at[gz],
            send_sem=back_send.at[to],
            recv_sem=back_recv.at[gz],
            device_id=(gy, to),
            device_id_type=MESH,
        )

    for k in sorted(range(SEGS), key=lambda k: -hops(k)):
        to = lax.rem(gz + k, SEGS)
        if k:
            back_copy(to).start()
    got_back[gz] = send_back[gz]

    for k, hf in ORDER:
        to = 2 * lax.rem(tile + k, 16) + hf
        if k:
            own_copy(to, hf).wait_send()
        else:

            @pl.when(half != hf)
            def _():
                own_copy(to, hf).wait_send()

        edge_copy(to, hf).wait_send()

    for k in range(1, SEGS):
        s = lax.rem(gz + k, SEGS)
        pltpu.make_async_copy(send_back.at[0], send_back.at[0], back_recv.at[s]).wait()

    low8 = win[:8] < 8
    for hf in (0, 1):
        parts = []
        for t in range(8):
            e = got_back[4 * t + hf]
            o = got_back[4 * t + 2 + hf]
            parts.append(jnp.where(low8, roll_l(e, -4), roll_l(o, 4)))
        for z, f in enumerate(swap_blocks(parts, blk[:8])):
            o_ref[z, pl.ds(8 * hf, 8)] = v_ref[z, pl.ds(8 * hf, 8)] + f

    for k in range(1, SEGS):
        s = lax.rem(gz + k, SEGS)
        pltpu.make_async_copy(send_back.at[0], send_back.at[0], back_send.at[s]).wait()


def body(electric_level, impurity_atoms, cell_materials):
    line = pltpu.VMEM((32, 16, 128), F32)
    vmem = pl.BlockSpec(memory_space=pltpu.VMEM)
    return pl.pallas_call(
        kernel,
        out_shape=jax.ShapeDtypeStruct(electric_level.shape, F32),
        in_specs=[pl.BlockSpec(memory_space=pltpu.HBM)] * 3,
        out_specs=vmem,
        scratch_shapes=[
            pltpu.VMEM(electric_level.shape, F32),
            pltpu.VMEM(electric_level.shape, jnp.int32),
            pltpu.VMEM(electric_level.shape, jnp.int32),
            pltpu.SemaphoreType.DMA((3,)),
            pltpu.VMEM((16, 3, 16, 128), F32),
            pltpu.VMEM((SEGS, 3, 16, 128), F32),
            pltpu.VMEM((SEGS, 8, 128), F32),
            pltpu.VMEM((SEGS, 8, 128), F32),
            pltpu.VMEM((3, 33, 16, 128), F32),
        ]
        + [line] * 18
        + [pltpu.SemaphoreType.DMA((SEGS,))] * 6,
        compiler_params=pltpu.CompilerParams(
            collective_id=0, has_side_effects=True, vmem_limit_bytes=32 * 1024 * 1024
        ),
        cost_estimate=pl.CostEstimate(flops=20_000_000, bytes_accessed=262144, transcendentals=200_000),
        name="newton_step",
    )(electric_level, impurity_atoms, cell_materials)


def solution(mesh):
    placed = P("gz", "gy", None)
    return jax.shard_map(
        body, mesh=mesh, in_specs=(placed,) * 3, out_specs=placed, check_vma=False
    )
```

```python
import jax
import jax.numpy as jnp
from jax import lax
from jax.experimental import pallas as pl
from jax.experimental.pallas import tpu as pltpu
from jax.sharding import PartitionSpec as P

MESH = pl.DeviceIdType.MESH
ZW = 8192.0
SEGS = 32
GYS = 16
F32 = jnp.float32


def hops(k):
    x, z = k // 8, k % 8
    return min(x, 4 - x) + min(z, 8 - z)


FAR_FIRST = sorted(range(SEGS), key=lambda k: -hops(k))
TILES_FAR_FIRST = sorted(range(16), key=lambda k: -hops(2 * k))


def roll_l(v, s):
    return pltpu.roll(v, s % 128, 1)


def roll_r(v, s):
    return pltpu.roll(v, s % 16, 0)


def swap_blocks(rows, blk):
    rows = list(rows)
    for bit in (1, 2, 4):
        keep = (blk & bit) == 0
        for i in range(8):
            if not i & bit:
                a, c = rows[i], rows[i | bit]
                rows[i] = jnp.where(keep, a, roll_l(c, 16 * bit))
                rows[i | bit] = jnp.where(keep, roll_l(a, -16 * bit), c)
    return rows


def face(a, b):
    total = a + b
    prod = a * b
    return jnp.where(prod > 0, 2.0 * prod / total, total)


MAIN = ((0, 4, 8), (8, 4, 8))
LOWER = (13, 1, 3)
UPPER = (0, 12, 3)
FORWARD = ((9, 1, 3), (4, 12, 3))
FIELDS = ((0, 2), (2, 1))


def eliminate(cond, excess, first_link, inv_ref, m_ref, h_ref, blk):
    zero = jnp.zeros_like(first_link)

    def step(i, carry):
        link_a, in_a, g_l, link_b, in_b, g_r = carry
        j = 30 - i
        g = excess[i] + in_a
        k = cond[i]
        inv = 1.0 / (link_a + k + g)
        m = k * inv
        h = link_a * inv
        inv_ref[i] = inv
        m_ref[i] = m
        h_ref[i] = h
        gb = excess[j] + in_b
        kb = cond[j - 1]
        invb = 1.0 / (link_b + kb + gb)
        mb = kb * invb
        hb = link_b * invb
        inv_ref[j] = invb
        m_ref[j] = mb
        h_ref[j] = hb
        return (link_a * m, g * m, g_l + g * h, link_b * mb, gb * mb, g_r + gb * hb)

    link_a, in_a, g_l, link_b, in_b, g_r = lax.fori_loop(
        0, 15, step, (first_link, zero, zero, cond[30], zero, zero), unroll=True
    )
    g = excess[15] + in_a + in_b
    inv = 1.0 / (link_a + link_b + g)
    ha = link_a * inv
    hb = link_b * inv
    inv_ref[15] = inv
    h_ref[15] = ha
    m_ref[15] = hb
    low = link_a * hb
    g_l = g_l + ha * g
    g_r = g_r + hb * g
    ground = excess[31] + g_r + roll_l(g_l, -16)
    up = roll_l(low, -16)
    factors = []
    for s in (16, 32, 64):
        inv = 1.0 / (low + up + ground)
        alpha = low * roll_l(inv, s)
        beta = up * roll_l(inv, -s)
        ground, low, up = (
            ground + alpha * roll_l(ground, s) + beta * roll_l(ground, -s),
            alpha * roll_l(low, s),
            beta * roll_l(up, -s),
        )
        factors.append((s, alpha, beta))
    return factors, 1.0 / ground


def line_solve(rhs, factors, inv_ref, m_ref, h_ref, b_ref, x_ref):
    seps, inv_sep = factors
    zero = jnp.zeros_like(inv_sep)

    def forward(i, carry):
        in_a, b_l, in_b, b_r = carry
        j = 30 - i
        b = rhs[i] + in_a
        bb = rhs[j] + in_b
        b_ref[i] = b
        b_ref[j] = bb
        return (m_ref[i] * b, b_l + h_ref[i] * b, m_ref[j] * bb, b_r + h_ref[j] * bb)

    in_a, b_l, in_b, b_r = lax.fori_loop(0, 15, forward, (zero, zero, zero, zero), unroll=True)
    mid = rhs[15] + in_a + in_b
    b_l = b_l + h_ref[15] * mid
    b_r = b_r + m_ref[15] * mid
    b = rhs[31] + b_r + roll_l(b_l, -16)
    for s, alpha, beta in seps:
        b = b + alpha * roll_l(b, s) + beta * roll_l(b, -s)
    x_r = b * inv_sep
    x_l = roll_l(x_r, 16)
    x_ref[31] = x_r
    mid = inv_ref[15] * mid + h_ref[15] * x_l + m_ref[15] * x_r
    x_ref[15] = mid

    def backward(n, carry):
        x_a, x_b = carry
        i = 14 - n
        j = 16 + n
        x_a = m_ref[i] * x_a + (inv_ref[i] * b_ref[i] + h_ref[i] * x_l)
        x_b = m_ref[j] * x_b + (inv_ref[j] * b_ref[j] + h_ref[j] * x_r)
        x_ref[i] = x_a
        x_ref[j] = x_b
        return (x_a, x_b)

    lax.fori_loop(0, 15, backward, (mid, mid), unroll=True)


def kernel(
    v_hbm, imp_hbm, mat_hbm, o_ref,
    v_ref, imp_ref, mat_ref, in_sem, pack, recv, send_back, got_back, grid,
    cond, excess, rhs0, rhs1, fx, fy, ccond, cexcess, inv, m, h, cinv, cm, ch, bb, x0, x1, xc,
    main_send, edge_send, main_recv, edge_recv, fwd_send, fwd_recv, back_send, back_recv,
):
    gy, gz = lax.axis_index("gy"), lax.axis_index("gz")
    core, par, tile = lax.rem(gy, 2), lax.rem(gz, 2), gz // 2
    chip = gy - core
    strip = chip + par
    edge_from = lax.rem(strip + GYS - 1 + 2 * core, GYS)

    fetch = [
        pltpu.make_async_copy(v_hbm, v_ref, in_sem.at[0]),
        pltpu.make_async_copy(mat_hbm, mat_ref, in_sem.at[1]),
        pltpu.make_async_copy(imp_hbm, imp_ref, in_sem.at[2]),
    ]
    for copy in fetch:
        copy.start()

    def hello(*device):
        pl.semaphore_signal(barrier, 1, device_id=device, device_id_type=MESH)

    barrier = pltpu.get_barrier_semaphore()
    for k in FAR_FIRST:
        other = lax.rem(gz + k, SEGS)
        if k:
            hello(strip, other)
            hello(edge_from, other)
        else:

            @pl.when(strip != gy)
            def _():
                hello(strip, other)

            @pl.when(edge_from != gy)
            def _():
                hello(edge_from, other)

            hello(chip + 1 - core, gz)

    lane = lax.broadcasted_iota(jnp.int32, (16, 128), 1)
    row = lax.broadcasted_iota(jnp.int32, (16, 128), 0)
    blk = lane // 16
    win = lax.rem(lane, 16)

    for copy in fetch:
        copy.wait()

    for a in range(3):
        for odd in (0, 1):
            planes = []
            for z in range(8):
                v = v_ref[z]
                mat = mat_ref[z]
                if a == 0:
                    f = v
                elif a == 1:
                    f = jnp.where(mat == 0, 1.0, jnp.where(mat == 1, 0.33, 0.64)).astype(F32)
                else:
                    charge = 0.5 * imp_ref[z].astype(F32) - 1.5
                    f = jnp.where(mat == 0, jnp.exp(v) - jnp.exp(-v) - charge, 0.0)
                planes.append(roll_l(f, -4 if odd else 4))
            for t, f in enumerate(swap_blocks(planes, blk)):
                pack[2 * t + odd, a] = f

    pl.semaphore_wait(barrier, 2 * SEGS)

    def copy_of(part, j, rows, device, send, got):
        a, n = FIELDS[part]
        src, dst, count = rows
        return pltpu.make_async_remote_copy(
            src_ref=pack.at[j, pl.ds(a, n), pl.ds(src, count)],
            dst_ref=recv.at[gz // 4, lax.rem(gz, 4), pl.ds(a, n), pl.ds(dst, count)],
            send_sem=send,
            recv_sem=got,
            device_id=device,
            device_id_type=MESH,
        )

    def main_copy(part, k, to_core):
        j = lax.rem(tile + k, 16)
        return copy_of(
            part, j, MAIN[to_core], (chip + to_core, 2 * j + core),
            main_send.at[part, to_core, k], main_recv.at[part, gz],
        )

    def edge_copy(part, k, upper):
        j = lax.rem(tile + k, 16)
        to = lax.rem(gy + core + (GYS - 1 if upper else 0), GYS)
        return copy_of(
            part, j, UPPER if upper else LOWER, (to, 2 * j + 1 - core),
            edge_send.at[part, upper, k], edge_recv.at[part, gz],
        )

    def keep(part, rows, got):
        a, n = FIELDS[part]
        src, dst, count = rows
        pltpu.make_async_copy(
            pack.at[tile, pl.ds(a, n), pl.ds(src, count)],
            recv.at[gz // 4, lax.rem(gz, 4), pl.ds(a, n), pl.ds(dst, count)],
            got.at[part, gz],
        ).start()

    main_self = [(par == core) & (core == to_core) for to_core in (0, 1)]
    edge_self = [(core == 0) & (par == 1), (core == 1) & (par == 0)]

    for part in (0, 1):
        for k in TILES_FAR_FIRST:
            for w in (0, 1):
                if k:
                    main_copy(part, k, w).start()
                    edge_copy(part, k, w).start()
                else:

                    @pl.when(main_self[w])
                    def _():
                        keep(part, MAIN[w], main_recv)

                    @pl.when(jnp.logical_not(main_self[w]))
                    def _():
                        main_copy(part, k, w).start()

                    @pl.when(edge_self[w])
                    def _():
                        keep(part, UPPER if w else LOWER, edge_recv)

                    @pl.when(jnp.logical_not(edge_self[w]))
                    def _():
                        edge_copy(part, k, w).start()

    y = strip * 16 + core * 8 - 4 + row
    x = tile * 8 - 4 + win
    inside = (row >= 1) & (row <= 14) & (y >= 0) & (y < GYS * 16) & (x >= 0) & (x < 128)
    odd_cell = lax.rem(row + win, 2) == 1
    colour0 = inside & jnp.logical_not(odd_cell)
    colour1 = inside & odd_cell

    def forward_copy(part, q, frm):
        a, n = FIELDS[part]
        src, dst, count = FORWARD[frm]
        return pltpu.make_async_remote_copy(
            src_ref=recv.at[:, q, pl.ds(a, n), pl.ds(src, count)],
            dst_ref=recv.at[:, q, pl.ds(a, n), pl.ds(dst, count)],
            send_sem=fwd_send.at[part, q],
            recv_sem=fwd_recv.at[part, q],
            device_id=(chip + 1 - frm, gz),
            device_id_type=MESH,
        )

    def forward(part):
        a, n = FIELDS[part]
        for q in range(4):
            for c in range(8):
                s = 4 * c + q
                for count, sem in ((8, main_recv), (3, edge_recv)):
                    piece = recv.at[0, 0, pl.ds(a, n), pl.ds(4, count)]
                    pltpu.make_async_copy(piece, piece, sem.at[part, s]).wait()
            for frm in (0, 1):

                @pl.when(core == frm)
                def _():
                    forward_copy(part, q, frm).start()

    def forwarded(part, q):
        a, n = FIELDS[part]
        piece = recv.at[:, 0, pl.ds(a, n), pl.ds(4, 3)]
        pltpu.make_async_copy(piece, piece, fwd_recv.at[part, q]).wait()

    forward(0)
    for q in range(4):
        forwarded(0, q)
        for a in range(2):
            parts = swap_blocks([recv[c, q, a] for c in range(8)], blk)
            for z in range(8):
                grid[a, 8 * q + z] = jnp.where(inside, parts[z], 0.0)

    for a in range(2):
        grid[a, 32] = jnp.where(blk == 7, 0.0, roll_l(grid[a, 0], -16))

    k_last = ZW * face(grid[1, 31], grid[1, 32])
    flow_last = k_last * (grid[0, 32] - grid[0, 31])
    k_floor = ZW * grid[1, 0]
    at_floor = blk == 0
    first_link = jnp.where(at_floor, 0.0, roll_l(k_last, 16))
    flow_first = jnp.where(at_floor, k_floor * grid[0, 0], roll_l(flow_last, 16))
    outside_one = jnp.where(inside, 0.0, 1.0)

    def assemble(i, flow_below):
        v = grid[0, i]
        p = grid[1, i]
        kz = ZW * face(p, grid[1, i + 1])
        flow = kz * (grid[0, i + 1] - v)
        px = face(p, roll_l(p, -1))
        py = face(p, roll_r(p, -1))
        flow_x = px * (roll_l(v, -1) - v)
        flow_y = py * (roll_r(v, -1) - v)
        soft = jnp.where(p == 1.0, jnp.exp(v) + jnp.exp(-v), 0.0) + outside_one
        extra = (px + roll_l(px, 1)) + (py + roll_r(py, 1)) + soft
        rhs0[i] = (flow - flow_below) + (flow_x - roll_l(flow_x, 1)) + (flow_y - roll_r(flow_y, 1))
        cond[i] = kz
        excess[i] = extra
        fx[i] = px
        fy[i] = py
        k2 = kz + roll_l(kz, -1)
        ccond[i] = k2 + roll_r(k2, -1)
        e2 = extra + roll_l(extra, -1) - 2.0 * px
        y2 = py + roll_l(py, -1)
        cexcess[i] = e2 + roll_r(e2, -1) - 2.0 * y2
        return flow

    lax.fori_loop(0, 32, assemble, flow_first, unroll=32)

    def quad(f):
        f = f + roll_l(f, -1)
        return f + roll_r(f, -1)

    floor = jnp.where(at_floor, k_floor, 0.0)
    roof = jnp.where(blk == 7, k_last, 0.0)
    excess[0] = excess[0] + floor
    excess[31] = excess[31] + roof
    cexcess[0] = cexcess[0] + quad(floor)
    cexcess[31] = cexcess[31] + quad(roof)

    fine = eliminate(cond, excess, first_link, inv, m, h, blk)
    coarse = eliminate(ccond, cexcess, quad(first_link), cinv, cm, ch, blk)

    forward(1)
    for q in range(4):
        forwarded(1, q)
        parts = swap_blocks([recv[c, q, 2] for c in range(8)], blk)
        for z in range(8):
            force = rhs0[8 * q + z] - parts[z]
            rhs0[8 * q + z] = jnp.where(colour0, force, 0.0)
            rhs1[8 * q + z] = jnp.where(colour1, force, 0.0)

    line_solve(rhs0, fine, inv, m, h, bb, x0)

    def lateral(f, i):
        gx, gyy = fx[i], fy[i]
        return (gx * roll_l(f, -1) + roll_l(gx * f, 1)) + (gyy * roll_r(f, -1) + roll_r(gyy * f, 1))

    def side(i, carry):
        rhs1[i] = jnp.where(colour1, rhs1[i] + lateral(x0[i], i), 0.0)
        return carry

    lax.fori_loop(0, 32, side, 0, unroll=32)
    line_solve(rhs1, fine, inv, m, h, bb, x1)

    def restrict(i, carry):
        rhs0[i] = quad(jnp.where(colour0, lateral(x1[i], i), 0.0))
        return carry

    lax.fori_loop(0, 32, restrict, 0, unroll=32)
    line_solve(rhs0, coarse, cinv, cm, ch, bb, xc)

    even_x = lax.rem(lane, 2) == 0
    even_y = lax.rem(row, 2) == 0

    for q in range(4):
        parts = []
        for z in range(8):
            i = 8 * q + z
            f = xc[i]
            f = jnp.where(even_x, f, roll_l(f, 1))
            f = jnp.where(even_y, f, roll_r(f, 1))
            parts.append((x0[i] + x1[i] + f)[4:12])
        for c, f in enumerate(swap_blocks(parts, blk[:8])):
            send_back[4 * c + q] = f

    slot = core * 16 + tile

    def back_copy(to):
        return pltpu.make_async_remote_copy(
            src_ref=send_back.at[to],
            dst_ref=got_back.at[slot],
            send_sem=back_send.at[to],
            recv_sem=back_recv.at[slot],
            device_id=(strip, to),
            device_id_type=MESH,
        )

    for k in FAR_FIRST:
        to = lax.rem(gz + k, SEGS)
        if k:
            back_copy(to).start()
        else:

            @pl.when(strip == gy)
            def _():
                pltpu.make_async_copy(
                    send_back.at[gz], got_back.at[slot], back_recv.at[slot]
                ).start()

            @pl.when(strip != gy)
            def _():
                back_copy(to).start()

    for part in (0, 1):
        for k in range(16):
            for w in (0, 1):
                if k:
                    main_copy(part, k, w).wait_send()
                    edge_copy(part, k, w).wait_send()
                else:

                    @pl.when(jnp.logical_not(main_self[w]))
                    def _():
                        main_copy(part, k, w).wait_send()

                    @pl.when(jnp.logical_not(edge_self[w]))
                    def _():
                        edge_copy(part, k, w).wait_send()

        for q in range(4):
            for frm in (0, 1):

                @pl.when(core == frm)
                def _():
                    forward_copy(part, q, frm).wait_send()

    for k in range(SEGS):
        pltpu.make_async_copy(send_back.at[0], send_back.at[0], back_recv.at[k]).wait()

    low8 = win[:8] < 8
    for to_core in (0, 1):
        parts = []
        for t in range(8):
            e = got_back[16 * to_core + 2 * t]
            o = got_back[16 * to_core + 2 * t + 1]
            parts.append(jnp.where(low8, roll_l(e, -4), roll_l(o, 4)))
        for z, f in enumerate(swap_blocks(parts, blk[:8])):
            o_ref[z, pl.ds(8 * to_core, 8)] = v_ref[z, pl.ds(8 * to_core, 8)] + f

    for k in range(SEGS):
        if k:
            to = lax.rem(gz + k, SEGS)
            back_copy(to).wait_send()
        else:

            @pl.when(strip != gy)
            def _():
                back_copy(gz).wait_send()


def body(electric_level, impurity_atoms, cell_materials):
    fields = (electric_level, impurity_atoms, cell_materials)
    line = pltpu.VMEM((32, 16, 128), F32)
    vmem = pl.BlockSpec(memory_space=pltpu.VMEM)
    return pl.pallas_call(
        kernel,
        out_shape=jax.ShapeDtypeStruct(electric_level.shape, F32),
        in_specs=[pl.BlockSpec(memory_space=pltpu.HBM)] * 3,
        out_specs=vmem,
        scratch_shapes=[
            pltpu.VMEM(electric_level.shape, F32),
            pltpu.VMEM(electric_level.shape, jnp.int32),
            pltpu.VMEM(electric_level.shape, jnp.int32),
            pltpu.SemaphoreType.DMA((3,)),
            pltpu.VMEM((16, 3, 16, 128), F32),
            pltpu.VMEM((8, 4, 3, 16, 128), F32),
            pltpu.VMEM((SEGS, 8, 128), F32),
            pltpu.VMEM((SEGS, 8, 128), F32),
            pltpu.VMEM((2, 33, 16, 128), F32),
        ]
        + [line] * 18
        + [pltpu.SemaphoreType.DMA((2, 2, 16))] * 2
        + [pltpu.SemaphoreType.DMA((2, SEGS))] * 2
        + [pltpu.SemaphoreType.DMA((2, 4))] * 2
        + [pltpu.SemaphoreType.DMA((SEGS,))] * 2,
        compiler_params=pltpu.CompilerParams(
            collective_id=0, has_side_effects=True, vmem_limit_bytes=32 * 1024 * 1024
        ),
        cost_estimate=pl.CostEstimate(flops=20_000_000, bytes_accessed=262144, transcendentals=200_000),
        name="newton_step",
    )(*(pltpu.with_memory_space_constraint(f, pltpu.HBM) for f in fields))


def solution(mesh):
    placed = P("gz", "gy", None)
    return jax.shard_map(
        body, mesh=mesh, in_specs=(placed,) * 3, out_specs=placed, check_vma=False
    )
```

```python
import jax
import jax.numpy as jnp
from jax import lax
from jax.experimental import pallas as pl
from jax.experimental.pallas import tpu as pltpu
from jax.sharding import PartitionSpec as P

MESH = pl.DeviceIdType.MESH
ZW = 8192.0
SEGS = 32
GYS = 16
F32 = jnp.float32


def hops(k):
    x, z = k // 8, k % 8
    return min(x, 4 - x) + min(z, 8 - z)


FAR_FIRST = sorted(range(SEGS), key=lambda k: -hops(k))
WIDE = 10
TILES = 13
OWNERS = 2 * TILES
TILES_FAR_FIRST = sorted(range(TILES), key=lambda k: -hops((SEGS * k // TILES) % SEGS))


def owner_place(n):
    return (16 * n) // TILES


def roll_l(v, s):
    return pltpu.roll(v, s % 128, 1)


def roll_r(v, s):
    return pltpu.roll(v, s % 16, 0)


def swap_blocks(rows, blk):
    rows = list(rows)
    for bit in (1, 2, 4):
        keep = (blk & bit) == 0
        for i in range(8):
            if not i & bit:
                a, c = rows[i], rows[i | bit]
                rows[i] = jnp.where(keep, a, roll_l(c, 16 * bit))
                rows[i | bit] = jnp.where(keep, roll_l(a, -16 * bit), c)
    return rows


def face(a, b):
    total = a + b
    prod = a * b
    return jnp.where(prod > 0, 2.0 * prod / total, total)


MAIN = ((0, 4, 8), (8, 4, 8))
LOWER = ((13, 1, 3), (14, 2, 2))
UPPER = ((0, 12, 3), (0, 12, 2))
FORWARD = (((9, 1, 3), (4, 12, 3)), ((10, 2, 2), (4, 12, 2)))
FIELDS = ((0, 2), (2, 1))


def eliminate(cond, excess, first_link, inv_ref, m_ref, h_ref, blk):
    zero = jnp.zeros_like(first_link)

    def step(i, carry):
        link_a, in_a, g_l, link_b, in_b, g_r = carry
        j = 30 - i
        g = excess[i] + in_a
        k = cond[i]
        inv = 1.0 / (link_a + k + g)
        m = k * inv
        h = link_a * inv
        inv_ref[i] = inv
        m_ref[i] = m
        h_ref[i] = h
        gb = excess[j] + in_b
        kb = cond[j - 1]
        invb = 1.0 / (link_b + kb + gb)
        mb = kb * invb
        hb = link_b * invb
        inv_ref[j] = invb
        m_ref[j] = mb
        h_ref[j] = hb
        return (link_a * m, g * m, g_l + g * h, link_b * mb, gb * mb, g_r + gb * hb)

    link_a, in_a, g_l, link_b, in_b, g_r = lax.fori_loop(
        0, 15, step, (first_link, zero, zero, cond[30], zero, zero), unroll=True
    )
    g = excess[15] + in_a + in_b
    inv = 1.0 / (link_a + link_b + g)
    ha = link_a * inv
    hb = link_b * inv
    inv_ref[15] = inv
    h_ref[15] = ha
    m_ref[15] = hb
    low = link_a * hb
    g_l = g_l + ha * g
    g_r = g_r + hb * g
    ground = excess[31] + g_r + roll_l(g_l, -16)
    up = roll_l(low, -16)
    factors = []
    for s in (16, 32, 64):
        inv = 1.0 / (low + up + ground)
        alpha = low * roll_l(inv, s)
        beta = up * roll_l(inv, -s)
        ground, low, up = (
            ground + alpha * roll_l(ground, s) + beta * roll_l(ground, -s),
            alpha * roll_l(low, s),
            beta * roll_l(up, -s),
        )
        factors.append((s, alpha, beta))
    return factors, 1.0 / ground


def line_solve(rhs, factors, inv_ref, m_ref, h_ref, b_ref, x_ref):
    seps, inv_sep = factors
    zero = jnp.zeros_like(inv_sep)

    def forward(i, carry):
        in_a, b_l, in_b, b_r = carry
        j = 30 - i
        b = rhs[i] + in_a
        bb = rhs[j] + in_b
        b_ref[i] = b
        b_ref[j] = bb
        return (m_ref[i] * b, b_l + h_ref[i] * b, m_ref[j] * bb, b_r + h_ref[j] * bb)

    in_a, b_l, in_b, b_r = lax.fori_loop(0, 15, forward, (zero, zero, zero, zero), unroll=True)
    mid = rhs[15] + in_a + in_b
    b_l = b_l + h_ref[15] * mid
    b_r = b_r + m_ref[15] * mid
    b = rhs[31] + b_r + roll_l(b_l, -16)
    for s, alpha, beta in seps:
        b = b + alpha * roll_l(b, s) + beta * roll_l(b, -s)
    x_r = b * inv_sep
    x_l = roll_l(x_r, 16)
    x_ref[31] = x_r
    mid = inv_ref[15] * mid + h_ref[15] * x_l + m_ref[15] * x_r
    x_ref[15] = mid

    def backward(n, carry):
        x_a, x_b = carry
        i = 14 - n
        j = 16 + n
        x_a = m_ref[i] * x_a + (inv_ref[i] * b_ref[i] + h_ref[i] * x_l)
        x_b = m_ref[j] * x_b + (inv_ref[j] * b_ref[j] + h_ref[j] * x_r)
        x_ref[i] = x_a
        x_ref[j] = x_b
        return (x_a, x_b)

    lax.fori_loop(0, 15, backward, (mid, mid), unroll=True)


def kernel(
    v_hbm, imp_hbm, mat_hbm, o_ref,
    v_ref, imp_ref, mat_ref, in_sem, pack, recv, send_back, got_back, grid,
    cond, excess, rhs0, rhs1, fx, fy, ccond, cexcess, inv, m, h, cinv, cm, ch, bb, x0, x1, xc,
    main_send, edge_send, main_recv, edge_recv, fwd_send, fwd_recv, back_send, back_recv,
):
    gy, gz = lax.axis_index("gy"), lax.axis_index("gz")
    core = lax.rem(gy, 2)
    number = (TILES * gz + 15) // 16
    owner = (number < OWNERS) & (owner_place(number) == gz)
    par, tile = lax.rem(number, 2), lax.rem(number // 2, TILES)
    chip = gy - core
    strip = chip + par
    edge_from = lax.rem(strip + GYS - 1 + 2 * core, GYS)

    fetch = [
        pltpu.make_async_copy(v_hbm, v_ref, in_sem.at[0]),
        pltpu.make_async_copy(mat_hbm, mat_ref, in_sem.at[1]),
        pltpu.make_async_copy(imp_hbm, imp_ref, in_sem.at[2]),
    ]
    for copy in fetch:
        copy.start()

    def hello(*device):
        pl.semaphore_signal(barrier, 1, device_id=device, device_id_type=MESH)

    barrier = pltpu.get_barrier_semaphore()

    @pl.when(owner)
    def _():
        for k in FAR_FIRST:
            other = lax.rem(gz + k, SEGS)
            if k:
                hello(strip, other)
                hello(edge_from, other)
            else:

                @pl.when(strip != gy)
                def _():
                    hello(strip, other)

                @pl.when(edge_from != gy)
                def _():
                    hello(edge_from, other)

                hello(chip + 1 - core, gz)

    lane = lax.broadcasted_iota(jnp.int32, (16, 128), 1)
    row = lax.broadcasted_iota(jnp.int32, (16, 128), 0)
    blk = lane // 16
    win = lax.rem(lane, 16)

    for copy in fetch:
        copy.wait()

    def pack_field(a):
        planes = []
        for z in range(8):
            v = v_ref[z]
            mat = mat_ref[z]
            if a == 0:
                f = v
            elif a == 1:
                f = jnp.where(mat == 0, 1.0, jnp.where(mat == 1, 0.33, 0.64)).astype(F32)
            else:
                charge = 0.5 * imp_ref[z].astype(F32) - 1.5
                f = jnp.where(mat == 0, jnp.exp(v) - jnp.exp(-v) - charge, 0.0)
            planes.append(f)
        for j in range(TILES):
            out = roll_l(planes[7], 16 * 7 - WIDE * j + 3)
            for z in range(7):
                out = jnp.where(blk == z, roll_l(planes[z], 16 * z - WIDE * j + 3), out)
            pack[j, a] = out

    for a in range(3):
        pack_field(a)

    pl.semaphore_wait(barrier, 4 * TILES)

    def copy_of(part, j, rows, device, send, got):
        a, n = FIELDS[part]
        src, dst, count = rows
        return pltpu.make_async_remote_copy(
            src_ref=pack.at[j, pl.ds(a, n), pl.ds(src, count)],
            dst_ref=recv.at[gz // 4, lax.rem(gz, 4), pl.ds(a, n), pl.ds(dst, count)],
            send_sem=send,
            recv_sem=got,
            device_id=device,
            device_id_type=MESH,
        )

    def main_copy(part, k, to_core):
        j = lax.rem(tile + k, TILES)
        return copy_of(
            part, j, MAIN[to_core], (chip + to_core, owner_place(2 * j + core)),
            main_send.at[part, to_core, k], main_recv.at[part, gz],
        )

    def edge_copy(part, k, upper):
        j = lax.rem(tile + k, TILES)
        to = lax.rem(gy + core + (GYS - 1 if upper else 0), GYS)
        return copy_of(
            part, j, (UPPER if upper else LOWER)[part], (to, owner_place(2 * j + 1 - core)),
            edge_send.at[part, upper, k], edge_recv.at[part, gz],
        )

    def keep(part, rows, got):
        a, n = FIELDS[part]
        src, dst, count = rows
        pltpu.make_async_copy(
            pack.at[tile, pl.ds(a, n), pl.ds(src, count)],
            recv.at[gz // 4, lax.rem(gz, 4), pl.ds(a, n), pl.ds(dst, count)],
            got.at[part, gz],
        ).start()

    main_self = [owner & (par == core) & (core == to_core) for to_core in (0, 1)]
    edge_self = [owner & (core == 0) & (par == 1), owner & (core == 1) & (par == 0)]

    def start_all(part):
        for k in TILES_FAR_FIRST:
            for w in (0, 1):
                if k:
                    main_copy(part, k, w).start()
                    edge_copy(part, k, w).start()
                else:

                    @pl.when(main_self[w])
                    def _():
                        keep(part, MAIN[w], main_recv)

                    @pl.when(jnp.logical_not(main_self[w]))
                    def _():
                        main_copy(part, k, w).start()

                    @pl.when(edge_self[w])
                    def _():
                        keep(part, (UPPER if w else LOWER)[part], edge_recv)

                    @pl.when(jnp.logical_not(edge_self[w]))
                    def _():
                        edge_copy(part, k, w).start()

    def sent_all(part):
        for k in range(TILES):
            for w in (0, 1):
                if k:
                    main_copy(part, k, w).wait_send()
                    edge_copy(part, k, w).wait_send()
                else:

                    @pl.when(jnp.logical_not(main_self[w]))
                    def _():
                        main_copy(part, k, w).wait_send()

                    @pl.when(jnp.logical_not(edge_self[w]))
                    def _():
                        edge_copy(part, k, w).wait_send()

    slot = core * TILES + tile

    def back_copy(to):
        return pltpu.make_async_remote_copy(
            src_ref=send_back.at[to],
            dst_ref=got_back.at[slot],
            send_sem=back_send.at[to],
            recv_sem=back_recv.at[slot],
            device_id=(strip, to),
            device_id_type=MESH,
        )

    start_all(0)
    sent_all(0)
    start_all(1)

    @pl.when(owner)
    def _():
        y = strip * 16 + core * 8 - 4 + row
        x = tile * WIDE - 3 + win
        inside = (row >= 1) & (row <= 14) & (y >= 0) & (y < GYS * 16) & (x >= 0) & (x < 128)
        odd_cell = lax.rem(row + win, 2) == 1
        inner = inside & (row >= 2) & (row <= 13)
        colour0 = inner & odd_cell
        colour1 = inner & jnp.logical_not(odd_cell)

        def forward_copy(part, q, frm):
            a, n = FIELDS[part]
            src, dst, count = FORWARD[part][frm]
            return pltpu.make_async_remote_copy(
                src_ref=recv.at[:, q, pl.ds(a, n), pl.ds(src, count)],
                dst_ref=recv.at[:, q, pl.ds(a, n), pl.ds(dst, count)],
                send_sem=fwd_send.at[part, q],
                recv_sem=fwd_recv.at[part, q],
                device_id=(chip + 1 - frm, gz),
                device_id_type=MESH,
            )

        def forward(part):
            a, n = FIELDS[part]
            for q in range(4):
                for c in range(8):
                    s = 4 * c + q
                    for count, sem in ((8, main_recv), (LOWER[part][2], edge_recv)):
                        piece = recv.at[0, 0, pl.ds(a, n), pl.ds(4, count)]
                        pltpu.make_async_copy(piece, piece, sem.at[part, s]).wait()
                for frm in (0, 1):

                    @pl.when(core == frm)
                    def _():
                        forward_copy(part, q, frm).start()

        def forwarded(part, q):
            a, n = FIELDS[part]
            piece = recv.at[:, 0, pl.ds(a, n), pl.ds(4, LOWER[part][2])]
            pltpu.make_async_copy(piece, piece, fwd_recv.at[part, q]).wait()

        forward(0)
        for q in range(4):
            forwarded(0, q)
            for a in range(2):
                parts = swap_blocks([recv[c, q, a] for c in range(8)], blk)
                for z in range(8):
                    grid[a, 8 * q + z] = jnp.where(inside, parts[z], 0.0)

        for a in range(2):
            grid[a, 32] = jnp.where(blk == 7, 0.0, roll_l(grid[a, 0], -16))

        k_last = ZW * face(grid[1, 31], grid[1, 32])
        flow_last = k_last * (grid[0, 32] - grid[0, 31])
        k_floor = ZW * grid[1, 0]
        at_floor = blk == 0
        first_link = jnp.where(at_floor, 0.0, roll_l(k_last, 16))
        flow_first = jnp.where(at_floor, k_floor * grid[0, 0], roll_l(flow_last, 16))
        outside_one = jnp.where(inside, 0.0, 1.0)

        def assemble(i, flow_below):
            v = grid[0, i]
            p = grid[1, i]
            kz = ZW * face(p, grid[1, i + 1])
            flow = kz * (grid[0, i + 1] - v)
            px = face(p, roll_l(p, -1))
            py = face(p, roll_r(p, -1))
            flow_x = px * (roll_l(v, -1) - v)
            flow_y = py * (roll_r(v, -1) - v)
            soft = jnp.where(p == 1.0, jnp.exp(v) + jnp.exp(-v), 0.0) + outside_one
            extra = (px + roll_l(px, 1)) + (py + roll_r(py, 1)) + soft
            rhs0[i] = (flow - flow_below) + (flow_x - roll_l(flow_x, 1)) + (flow_y - roll_r(flow_y, 1))
            cond[i] = kz
            excess[i] = extra
            fx[i] = px
            fy[i] = py
            k2 = kz + roll_l(kz, -1)
            ccond[i] = k2 + roll_r(k2, -1)
            e2 = extra + roll_l(extra, -1) - 2.0 * px
            y2 = py + roll_l(py, -1)
            cexcess[i] = e2 + roll_r(e2, -1) - 2.0 * y2
            return flow

        lax.fori_loop(0, 32, assemble, flow_first, unroll=32)

        def quad(f):
            f = f + roll_l(f, -1)
            return f + roll_r(f, -1)

        floor = jnp.where(at_floor, k_floor, 0.0)
        roof = jnp.where(blk == 7, k_last, 0.0)
        excess[0] = excess[0] + floor
        excess[31] = excess[31] + roof
        cexcess[0] = cexcess[0] + quad(floor)
        cexcess[31] = cexcess[31] + quad(roof)

        fine = eliminate(cond, excess, first_link, inv, m, h, blk)
        coarse = eliminate(ccond, cexcess, quad(first_link), cinv, cm, ch, blk)

        forward(1)
        for q in range(4):
            forwarded(1, q)
            parts = swap_blocks([recv[c, q, 2] for c in range(8)], blk)
            for z in range(8):
                force = rhs0[8 * q + z] - parts[z]
                rhs0[8 * q + z] = jnp.where(colour0, force, 0.0)
                rhs1[8 * q + z] = jnp.where(colour1, force, 0.0)

        line_solve(rhs0, fine, inv, m, h, bb, x0)

        def lateral(f, i):
            gx, gyy = fx[i], fy[i]
            return (gx * roll_l(f, -1) + roll_l(gx * f, 1)) + (gyy * roll_r(f, -1) + roll_r(gyy * f, 1))

        def side(i, carry):
            rhs1[i] = jnp.where(colour1, rhs1[i] + lateral(x0[i], i), 0.0)
            return carry

        lax.fori_loop(0, 32, side, 0, unroll=32)
        line_solve(rhs1, fine, inv, m, h, bb, x1)

        def restrict(i, carry):
            rhs0[i] = quad(jnp.where(colour0, lateral(x1[i], i), 0.0))
            return carry

        lax.fori_loop(0, 32, restrict, 0, unroll=32)
        line_solve(rhs0, coarse, cinv, cm, ch, bb, xc)

        odd_x = lax.rem(lane, 2) == 1
        even_y = lax.rem(row, 2) == 0

        for q in range(4):
            parts = []
            for z in range(8):
                i = 8 * q + z
                f = xc[i]
                f = jnp.where(odd_x, f, roll_l(f, 1))
                f = jnp.where(even_y, f, roll_r(f, 1))
                parts.append((x0[i] + x1[i] + f)[4:12])
            for c, f in enumerate(swap_blocks(parts, blk[:8])):
                send_back[4 * c + q] = f


        for k in FAR_FIRST:
            to = lax.rem(gz + k, SEGS)
            if k:
                back_copy(to).start()
            else:

                @pl.when(strip == gy)
                def _():
                    pltpu.make_async_copy(
                        send_back.at[gz], got_back.at[slot], back_recv.at[slot]
                    ).start()

                @pl.when(strip != gy)
                def _():
                    back_copy(to).start()

        for part in (0, 1):
            for q in range(4):
                for frm in (0, 1):

                    @pl.when(core == frm)
                    def _():
                        forward_copy(part, q, frm).wait_send()

    sent_all(1)

    for k in range(OWNERS):
        pltpu.make_async_copy(send_back.at[0], send_back.at[0], back_recv.at[k]).wait()

    column = lane[:8] // WIDE
    for to_core in (0, 1):
        rows = pl.ds(8 * to_core, 8)
        for z in range(8):
            f = roll_l(got_back[to_core * TILES], -3 - 16 * z)
            for j in range(1, TILES):
                f = jnp.where(
                    column == j, roll_l(got_back[to_core * TILES + j], WIDE * j - 3 - 16 * z), f
                )
            o_ref[z, rows] = v_ref[z, rows] + f

    @pl.when(owner)
    def _():
        for k in range(SEGS):
            if k:
                back_copy(lax.rem(gz + k, SEGS)).wait_send()
            else:

                @pl.when(strip != gy)
                def _():
                    back_copy(gz).wait_send()


def body(electric_level, impurity_atoms, cell_materials):
    fields = (electric_level, impurity_atoms, cell_materials)
    line = pltpu.VMEM((32, 16, 128), F32)
    vmem = pl.BlockSpec(memory_space=pltpu.VMEM)
    return pl.pallas_call(
        kernel,
        out_shape=jax.ShapeDtypeStruct(electric_level.shape, F32),
        in_specs=[pl.BlockSpec(memory_space=pltpu.HBM)] * 3,
        out_specs=vmem,
        scratch_shapes=[
            pltpu.VMEM(electric_level.shape, F32),
            pltpu.VMEM(electric_level.shape, jnp.int32),
            pltpu.VMEM(electric_level.shape, jnp.int32),
            pltpu.SemaphoreType.DMA((3,)),
            pltpu.VMEM((TILES, 3, 16, 128), F32),
            pltpu.VMEM((8, 4, 3, 16, 128), F32),
            pltpu.VMEM((SEGS, 8, 128), F32),
            pltpu.VMEM((OWNERS, 8, 128), F32),
            pltpu.VMEM((2, 33, 16, 128), F32),
        ]
        + [line] * 18
        + [pltpu.SemaphoreType.DMA((2, 2, TILES))] * 2
        + [pltpu.SemaphoreType.DMA((2, SEGS))] * 2
        + [pltpu.SemaphoreType.DMA((2, 4))] * 2
        + [pltpu.SemaphoreType.DMA((SEGS,)), pltpu.SemaphoreType.DMA((OWNERS,))],
        compiler_params=pltpu.CompilerParams(
            collective_id=0, has_side_effects=True, vmem_limit_bytes=32 * 1024 * 1024
        ),
        cost_estimate=pl.CostEstimate(flops=20_000_000, bytes_accessed=262144, transcendentals=200_000),
        name="newton_step",
    )(*(pltpu.with_memory_space_constraint(f, pltpu.HBM) for f in fields))


def solution(mesh):
    placed = P("gz", "gy", None)
    return jax.shard_map(
        body, mesh=mesh, in_specs=(placed,) * 3, out_specs=placed, check_vma=False
    )
```

```python
import jax
import jax.numpy as jnp
from jax import lax
from jax.experimental import pallas as pl
from jax.experimental.pallas import tpu as pltpu
from jax.sharding import PartitionSpec as P

MESH = pl.DeviceIdType.MESH
ZW = 8192.0
SEGS = 32
GYS = 16
F32 = jnp.float32


def hops(k):
    x, z = k // 8, k % 8
    return min(x, 4 - x) + min(z, 8 - z)


FAR_FIRST = sorted(range(SEGS), key=lambda k: -hops(k))
WIDE = 10
TILES = 13
OWNERS = 2 * TILES
TILES_FAR_FIRST = sorted(range(TILES), key=lambda k: -hops((SEGS * k // TILES) % SEGS))


def owner_place(n):
    return (16 * n) // TILES


def roll_l(v, s):
    return pltpu.roll(v, s % 128, 1)


def roll_r(v, s):
    return pltpu.roll(v, s % 16, 0)


def swap_blocks(rows, blk):
    rows = list(rows)
    for bit in (1, 2, 4):
        keep = (blk & bit) == 0
        for i in range(8):
            if not i & bit:
                a, c = rows[i], rows[i | bit]
                rows[i] = jnp.where(keep, a, roll_l(c, 16 * bit))
                rows[i | bit] = jnp.where(keep, roll_l(a, -16 * bit), c)
    return rows


def face(a, b):
    total = a + b
    prod = a * b
    return jnp.where(prod > 0, 2.0 * prod / total, total)


MAIN = ((0, 0, 8), (8, 0, 8))
LOWER = ((13, 13, 3), (14, 14, 2))
UPPER = ((0, 8, 3), (0, 8, 2))
FORWARD = (((5, 13, 3), (0, 8, 3)), ((6, 14, 2), (0, 8, 2)))
FIELDS = ((0, 2), (2, 1))


def eliminate(cond, excess, first_link, inv_ref, m_ref, h_ref, blk):
    zero = jnp.zeros_like(first_link)

    def step(i, carry):
        link_a, in_a, g_l, link_b, in_b, g_r = carry
        j = 30 - i
        g = excess[i] + in_a
        k = cond[i]
        inv = 1.0 / (link_a + k + g)
        m = k * inv
        h = link_a * inv
        inv_ref[i] = inv
        m_ref[i] = m
        h_ref[i] = h
        gb = excess[j] + in_b
        kb = cond[j - 1]
        invb = 1.0 / (link_b + kb + gb)
        mb = kb * invb
        hb = link_b * invb
        inv_ref[j] = invb
        m_ref[j] = mb
        h_ref[j] = hb
        return (link_a * m, g * m, g_l + g * h, link_b * mb, gb * mb, g_r + gb * hb)

    link_a, in_a, g_l, link_b, in_b, g_r = lax.fori_loop(
        0, 15, step, (first_link, zero, zero, cond[30], zero, zero), unroll=True
    )
    g = excess[15] + in_a + in_b
    inv = 1.0 / (link_a + link_b + g)
    ha = link_a * inv
    hb = link_b * inv
    inv_ref[15] = inv
    h_ref[15] = ha
    m_ref[15] = hb
    low = link_a * hb
    g_l = g_l + ha * g
    g_r = g_r + hb * g
    ground = excess[31] + g_r + roll_l(g_l, -16)
    up = roll_l(low, -16)
    factors = []
    for s in (16, 32, 64):
        inv = 1.0 / (low + up + ground)
        alpha = low * roll_l(inv, s)
        beta = up * roll_l(inv, -s)
        ground, low, up = (
            ground + alpha * roll_l(ground, s) + beta * roll_l(ground, -s),
            alpha * roll_l(low, s),
            beta * roll_l(up, -s),
        )
        factors.append((s, alpha, beta))
    return factors, 1.0 / ground


def line_solve(rhs, factors, inv_ref, m_ref, h_ref, b_ref, x_ref):
    seps, inv_sep = factors
    zero = jnp.zeros_like(inv_sep)

    def forward(i, carry):
        in_a, b_l, in_b, b_r = carry
        j = 30 - i
        b = rhs[i] + in_a
        bb = rhs[j] + in_b
        b_ref[i] = b
        b_ref[j] = bb
        return (m_ref[i] * b, b_l + h_ref[i] * b, m_ref[j] * bb, b_r + h_ref[j] * bb)

    in_a, b_l, in_b, b_r = lax.fori_loop(0, 15, forward, (zero, zero, zero, zero), unroll=True)
    mid = rhs[15] + in_a + in_b
    b_l = b_l + h_ref[15] * mid
    b_r = b_r + m_ref[15] * mid
    b = rhs[31] + b_r + roll_l(b_l, -16)
    for s, alpha, beta in seps:
        b = b + alpha * roll_l(b, s) + beta * roll_l(b, -s)
    x_r = b * inv_sep
    x_l = roll_l(x_r, 16)
    x_ref[31] = x_r
    mid = inv_ref[15] * mid + h_ref[15] * x_l + m_ref[15] * x_r
    x_ref[15] = mid

    def backward(n, carry):
        x_a, x_b = carry
        i = 14 - n
        j = 16 + n
        x_a = m_ref[i] * x_a + (inv_ref[i] * b_ref[i] + h_ref[i] * x_l)
        x_b = m_ref[j] * x_b + (inv_ref[j] * b_ref[j] + h_ref[j] * x_r)
        x_ref[i] = x_a
        x_ref[j] = x_b
        return (x_a, x_b)

    lax.fori_loop(0, 15, backward, (mid, mid), unroll=True)


def kernel(
    v_hbm, imp_hbm, mat_hbm, o_ref,
    v_ref, imp_ref, mat_ref, in_sem, pack, recv, send_back, got_back, grid,
    cond, excess, rhs0, rhs1, fx, fy, ccond, cexcess, inv, m, h, cinv, cm, ch, bb, x0, x1, xc, crhs, cbb,
    main_send, edge_send, arrived, fwd_send, fwd_recv, back_send, back_recv,
):
    gy, gz = lax.axis_index("gy"), lax.axis_index("gz")
    core = lax.rem(gy, 2)
    number = (TILES * gz + 15) // 16
    owner = (number < OWNERS) & (owner_place(number) == gz)
    par, tile = lax.rem(number, 2), lax.rem(number // 2, TILES)
    chip = gy - core
    strip = chip + par
    edge_from = lax.rem(strip + GYS - 1 + 2 * core, GYS)

    fetch = [
        pltpu.make_async_copy(v_hbm, v_ref, in_sem.at[0]),
        pltpu.make_async_copy(mat_hbm, mat_ref, in_sem.at[1]),
        pltpu.make_async_copy(imp_hbm, imp_ref, in_sem.at[2]),
    ]
    for copy in fetch:
        copy.start()

    def hello(*device):
        pl.semaphore_signal(barrier, 1, device_id=device, device_id_type=MESH)

    barrier = pltpu.get_barrier_semaphore()

    @pl.when(owner)
    def _():
        for k in FAR_FIRST:
            other = lax.rem(gz + k, SEGS)
            if k:
                hello(strip, other)
                hello(edge_from, other)
            else:

                @pl.when(strip != gy)
                def _():
                    hello(strip, other)

                @pl.when(edge_from != gy)
                def _():
                    hello(edge_from, other)

                hello(chip + 1 - core, gz)

    lane = lax.broadcasted_iota(jnp.int32, (16, 128), 1)
    row = lax.broadcasted_iota(jnp.int32, (16, 128), 0)
    blk = lane // 16
    win = lax.rem(lane, 16)

    for copy in fetch:
        copy.wait()

    def pack_field(a):
        planes = []
        for z in range(8):
            v = v_ref[z]
            mat = mat_ref[z]
            if a == 0:
                f = v
            elif a == 1:
                f = jnp.where(mat == 0, 1.0, jnp.where(mat == 1, 0.33, 0.64)).astype(F32)
            else:
                charge = 0.5 * imp_ref[z].astype(F32) - 1.5
                f = jnp.where(mat == 0, jnp.exp(v) - jnp.exp(-v) - charge, 0.0)
            planes.append(f)
        for j in range(TILES):
            out = roll_l(planes[7], 16 * 7 - WIDE * j + 3)
            for z in range(7):
                out = jnp.where(blk == z, roll_l(planes[z], 16 * z - WIDE * j + 3), out)
            pack[j, a] = out

    for a in range(3):
        pack_field(a)

    pl.semaphore_wait(barrier, 4 * TILES)

    def copy_of(part, j, rows, device, send, got):
        a, n = FIELDS[part]
        src, dst, count = rows
        return pltpu.make_async_remote_copy(
            src_ref=pack.at[j, pl.ds(a, n), pl.ds(src, count)],
            dst_ref=recv.at[gz // 4, lax.rem(gz, 4), pl.ds(a, n), pl.ds(dst, count)],
            send_sem=send,
            recv_sem=got,
            device_id=device,
            device_id_type=MESH,
        )

    def main_copy(part, k, to_core):
        j = lax.rem(tile + k, TILES)
        return copy_of(
            part, j, MAIN[to_core], (chip + to_core, owner_place(2 * j + core)),
            main_send.at[part, to_core, k], arrived.at[part, lax.rem(gz, 4)],
        )

    def edge_copy(part, k, upper):
        j = lax.rem(tile + k, TILES)
        to = lax.rem(gy + core + (GYS - 1 if upper else 0), GYS)
        return copy_of(
            part, j, (UPPER if upper else LOWER)[part], (to, owner_place(2 * j + 1 - core)),
            edge_send.at[part, upper, k], arrived.at[part, lax.rem(gz, 4)],
        )

    def keep(part, rows):
        a, n = FIELDS[part]
        src, dst, count = rows
        pltpu.make_async_copy(
            pack.at[tile, pl.ds(a, n), pl.ds(src, count)],
            recv.at[gz // 4, lax.rem(gz, 4), pl.ds(a, n), pl.ds(dst, count)],
            arrived.at[part, lax.rem(gz, 4)],
        ).start()

    main_self = [owner & (par == core) & (core == to_core) for to_core in (0, 1)]
    edge_self = [owner & (core == 0) & (par == 1), owner & (core == 1) & (par == 0)]

    def start_all(part):
        for k in TILES_FAR_FIRST:
            for w in (0, 1):
                if k:
                    main_copy(part, k, w).start()
                    edge_copy(part, k, w).start()
                else:

                    @pl.when(main_self[w])
                    def _():
                        keep(part, MAIN[w])

                    @pl.when(jnp.logical_not(main_self[w]))
                    def _():
                        main_copy(part, k, w).start()

                    @pl.when(edge_self[w])
                    def _():
                        keep(part, (UPPER if w else LOWER)[part])

                    @pl.when(jnp.logical_not(edge_self[w]))
                    def _():
                        edge_copy(part, k, w).start()

    def sent_all(part):
        for k in range(TILES):
            for w in (0, 1):
                if k:
                    main_copy(part, k, w).wait_send()
                    edge_copy(part, k, w).wait_send()
                else:

                    @pl.when(jnp.logical_not(main_self[w]))
                    def _():
                        main_copy(part, k, w).wait_send()

                    @pl.when(jnp.logical_not(edge_self[w]))
                    def _():
                        edge_copy(part, k, w).wait_send()

    slot = core * TILES + tile

    def back_copy(to):
        return pltpu.make_async_remote_copy(
            src_ref=send_back.at[to],
            dst_ref=got_back.at[slot],
            send_sem=back_send.at[to],
            recv_sem=back_recv.at[0],
            device_id=(strip, to),
            device_id_type=MESH,
        )

    start_all(0)
    sent_all(0)
    start_all(1)

    @pl.when(owner)
    def _():
        y = strip * 16 + core * 8 + jnp.where(row < 12, row, row - 16)
        x = tile * WIDE - 3 + win
        inside = ((row <= 10) | (row >= 13)) & (y >= 0) & (y < GYS * 16) & (x >= 0) & (x < 128)
        odd_cell = lax.rem(row + win, 2) == 1
        inner = inside & ((row <= 9) | (row >= 14))
        colour0 = inner & odd_cell
        colour1 = inner & jnp.logical_not(odd_cell)

        def forward_copy(part, q, frm):
            a, n = FIELDS[part]
            src, dst, count = FORWARD[part][frm]
            return pltpu.make_async_remote_copy(
                src_ref=recv.at[:, q, pl.ds(a, n), pl.ds(src, count)],
                dst_ref=recv.at[:, q, pl.ds(a, n), pl.ds(dst, count)],
                send_sem=fwd_send.at[part, q],
                recv_sem=fwd_recv.at[part, q],
                device_id=(chip + 1 - frm, gz),
                device_id_type=MESH,
            )

        def forward(part):
            a, n = FIELDS[part]
            for q in range(4):
                piece = recv.at[:, q, pl.ds(a, n), pl.ds(0, 8 + LOWER[part][2])]
                pltpu.make_async_copy(piece, piece, arrived.at[part, q]).wait()
                for frm in (0, 1):

                    @pl.when(core == frm)
                    def _():
                        forward_copy(part, q, frm).start()

        def forwarded(part, q):
            a, n = FIELDS[part]
            piece = recv.at[:, 0, pl.ds(a, n), pl.ds(0, LOWER[part][2])]
            pltpu.make_async_copy(piece, piece, fwd_recv.at[part, q]).wait()

        forward(0)
        for q in range(4):
            forwarded(0, q)
            for a in range(2):
                parts = swap_blocks([recv[c, q, a] for c in range(8)], blk)
                for z in range(8):
                    grid[a, 8 * q + z] = jnp.where(inside, parts[z], 0.0)

        for a in range(2):
            grid[a, 32] = jnp.where(blk == 7, 0.0, roll_l(grid[a, 0], -16))

        k_last = ZW * face(grid[1, 31], grid[1, 32])
        flow_last = k_last * (grid[0, 32] - grid[0, 31])
        k_floor = ZW * grid[1, 0]
        at_floor = blk == 0
        first_link = jnp.where(at_floor, 0.0, roll_l(k_last, 16))
        flow_first = jnp.where(at_floor, k_floor * grid[0, 0], roll_l(flow_last, 16))
        outside_one = jnp.where(inside, 0.0, 1.0)

        def quad(f):
            f = f + roll_l(f, -1)
            return f + pltpu.roll(f, 7, 0)

        def assemble(i, flow_below):
            v = grid[0, i]
            p = grid[1, i]
            kz = ZW * face(p, grid[1, i + 1])
            flow = kz * (grid[0, i + 1] - v)
            px = face(p, roll_l(p, -1))
            py = face(p, roll_r(p, -1))
            flow_x = px * (roll_l(v, -1) - v)
            flow_y = py * (roll_r(v, -1) - v)
            soft = jnp.where(p == 1.0, jnp.exp(v) + jnp.exp(-v), 0.0) + outside_one
            extra = (px + roll_l(px, 1)) + (py + roll_r(py, 1)) + soft
            rhs0[i] = (flow - flow_below) + (flow_x - roll_l(flow_x, 1)) + (flow_y - roll_r(flow_y, 1))
            cond[i] = kz
            excess[i] = extra
            fx[i] = px
            fy[i] = py
            ccond[i] = quad(kz[:8])
            e2 = extra[:8] + roll_l(extra[:8], -1) - 2.0 * px[:8]
            y2 = py[:8] + roll_l(py[:8], -1)
            cexcess[i] = e2 + pltpu.roll(e2, 7, 0) - 2.0 * y2
            return flow

        lax.fori_loop(0, 32, assemble, flow_first, unroll=32)

        floor = jnp.where(at_floor, k_floor, 0.0)
        roof = jnp.where(blk == 7, k_last, 0.0)
        excess[0] = excess[0] + floor
        excess[31] = excess[31] + roof
        cexcess[0] = cexcess[0] + quad(floor[:8])
        cexcess[31] = cexcess[31] + quad(roof[:8])

        fine = eliminate(cond, excess, first_link, inv, m, h, blk)
        coarse = eliminate(ccond, cexcess, quad(first_link[:8]), cinv, cm, ch, blk)

        forward(1)
        for q in range(4):
            forwarded(1, q)
            parts = swap_blocks([recv[c, q, 2] for c in range(8)], blk)
            for z in range(8):
                force = rhs0[8 * q + z] - parts[z]
                rhs0[8 * q + z] = jnp.where(colour0, force, 0.0)
                rhs1[8 * q + z] = jnp.where(colour1, force, 0.0)

        line_solve(rhs0, fine, inv, m, h, bb, x0)

        def lateral(f, i):
            gx, gyy = fx[i], fy[i]
            return (gx * roll_l(f, -1) + roll_l(gx * f, 1)) + (gyy * roll_r(f, -1) + roll_r(gyy * f, 1))

        def side(i, carry):
            rhs1[i] = jnp.where(colour1, rhs1[i] + lateral(x0[i], i), 0.0)
            return carry

        lax.fori_loop(0, 32, side, 0, unroll=32)
        line_solve(rhs1, fine, inv, m, h, bb, x1)

        def restrict(i, carry):
            f = x1[i]
            g = fy[i] * f
            gx, gyy, t = fx[i, :8], fy[i, :8], f[:8]
            out = (gx * roll_l(t, -1) + roll_l(gx * t, 1)) + (
                gyy * roll_r(f, -1)[:8] + roll_r(g, 1)[:8]
            )
            crhs[i] = quad(jnp.where(colour0[:8], out, 0.0))
            return carry

        lax.fori_loop(0, 32, restrict, 0, unroll=32)
        line_solve(crhs, coarse, cinv, cm, ch, cbb, xc)

        odd_x = lax.rem(lane, 2) == 1
        even_y = lax.rem(row, 2) == 0

        for q in range(4):
            parts = []
            for z in range(8):
                i = 8 * q + z
                f = xc[i]
                f = jnp.where(odd_x[:8], f, roll_l(f, 1))
                f = jnp.where(even_y[:8], f, pltpu.roll(f, 1, 0))
                parts.append(x0[i, :8] + x1[i, :8] + f)
            for c, f in enumerate(swap_blocks(parts, blk[:8])):
                send_back[4 * c + q] = f


        for k in FAR_FIRST:
            to = lax.rem(gz + k, SEGS)
            if k:
                back_copy(to).start()
            else:

                @pl.when(strip == gy)
                def _():
                    pltpu.make_async_copy(
                        send_back.at[gz], got_back.at[slot], back_recv.at[0]
                    ).start()

                @pl.when(strip != gy)
                def _():
                    back_copy(to).start()

        for part in (0, 1):
            for q in range(4):
                for frm in (0, 1):

                    @pl.when(core == frm)
                    def _():
                        forward_copy(part, q, frm).wait_send()

    sent_all(1)

    pltpu.make_async_copy(got_back, got_back, back_recv.at[0]).wait()

    column = lane[:8] // WIDE
    for to_core in (0, 1):
        rows = pl.ds(8 * to_core, 8)
        for z in range(8):
            f = roll_l(got_back[to_core * TILES], -3 - 16 * z)
            for j in range(1, TILES):
                f = jnp.where(
                    column == j, roll_l(got_back[to_core * TILES + j], WIDE * j - 3 - 16 * z), f
                )
            o_ref[z, rows] = v_ref[z, rows] + f

    @pl.when(owner)
    def _():
        for k in range(SEGS):
            if k:
                back_copy(lax.rem(gz + k, SEGS)).wait_send()
            else:

                @pl.when(strip != gy)
                def _():
                    back_copy(gz).wait_send()


def body(electric_level, impurity_atoms, cell_materials):
    fields = (electric_level, impurity_atoms, cell_materials)
    line = pltpu.VMEM((32, 16, 128), F32)
    half = pltpu.VMEM((32, 8, 128), F32)
    vmem = pl.BlockSpec(memory_space=pltpu.VMEM)
    return pl.pallas_call(
        kernel,
        out_shape=jax.ShapeDtypeStruct(electric_level.shape, F32),
        in_specs=[pl.BlockSpec(memory_space=pltpu.HBM)] * 3,
        out_specs=vmem,
        scratch_shapes=[
            pltpu.VMEM(electric_level.shape, F32),
            pltpu.VMEM(electric_level.shape, jnp.int32),
            pltpu.VMEM(electric_level.shape, jnp.int32),
            pltpu.SemaphoreType.DMA((3,)),
            pltpu.VMEM((TILES, 3, 16, 128), F32),
            pltpu.VMEM((8, 4, 3, 16, 128), F32),
            pltpu.VMEM((SEGS, 8, 128), F32),
            pltpu.VMEM((OWNERS, 8, 128), F32),
            pltpu.VMEM((2, 33, 16, 128), F32),
        ]
        + [line] * 6
        + [half] * 2
        + [line] * 3
        + [half] * 3
        + [line] * 3
        + [half] * 3
        + [pltpu.SemaphoreType.DMA((2, 2, TILES))] * 2
        + [pltpu.SemaphoreType.DMA((2, 4))] * 3
        + [pltpu.SemaphoreType.DMA((SEGS,)), pltpu.SemaphoreType.DMA((1,))],
        compiler_params=pltpu.CompilerParams(
            collective_id=0, has_side_effects=True, vmem_limit_bytes=32 * 1024 * 1024
        ),
        cost_estimate=pl.CostEstimate(flops=20_000_000, bytes_accessed=262144, transcendentals=200_000),
        name="newton_step",
    )(*(pltpu.with_memory_space_constraint(f, pltpu.HBM) for f in fields))


def solution(mesh):
    placed = P("gz", "gy", None)
    return jax.shard_map(
        body, mesh=mesh, in_specs=(placed,) * 3, out_specs=placed, check_vma=False
    )
```

```python
import jax
import jax.numpy as jnp
from jax import lax
from jax.experimental import pallas as pl
from jax.experimental.pallas import tpu as pltpu
from jax.sharding import PartitionSpec as P

MESH = pl.DeviceIdType.MESH
ZW = 8192.0
SEGS = 32
GYS = 16
F32 = jnp.float32


def hops(k):
    x, z = k // 8, k % 8
    return min(x, 4 - x) + min(z, 8 - z)


FAR_FIRST = sorted(range(SEGS), key=lambda k: -hops(k))
WIDE = 10
TILES = 13
OWNERS = 2 * TILES
TILES_FAR_FIRST = sorted(range(TILES), key=lambda k: -hops((SEGS * k // TILES) % SEGS))


def owner_place(n):
    return (16 * n) // TILES


def roll_l(v, s):
    return pltpu.roll(v, s % 128, 1) if s % 128 else v


def roll_r(v, s):
    return pltpu.roll(v, s % 16, 0)


def swap_blocks(rows, blk):
    rows = list(rows)
    for bit in (1, 2, 4):
        keep = (blk & bit) == 0
        for i in range(8):
            if not i & bit:
                a, c = rows[i], rows[i | bit]
                rows[i] = jnp.where(keep, a, roll_l(c, 16 * bit))
                rows[i | bit] = jnp.where(keep, roll_l(a, -16 * bit), c)
    return rows


def face(a, b):
    total = a + b
    prod = a * b
    return jnp.where(prod > 0, 2.0 * prod / total, total)


MAIN = (((0, 0, 8), (8, 0, 8)), ((0, 0, 10), (8, 0, 8)))
INNER = (6, 14, 2)
LOWER = ((13, 13, 3), (14, 14, 2))
UPPER = ((0, 8, 3), (0, 8, 2))
FORWARD = ((5, 13, 3), (0, 8, 3))
ROWS = (11, 12)
FIELDS = ((0, 2), (2, 1))


def eliminate(cond, excess, first_link, inv_ref, m_ref, h_ref, blk):
    zero = jnp.zeros_like(first_link)

    def step(i, carry):
        link_a, in_a, g_l, link_b, in_b, g_r = carry
        j = 30 - i
        g = excess[i] + in_a
        k = cond[i]
        inv = 1.0 / (link_a + k + g)
        m = k * inv
        h = link_a * inv
        inv_ref[i] = inv
        m_ref[i] = m
        h_ref[i] = h
        gb = excess[j] + in_b
        kb = cond[j - 1]
        invb = 1.0 / (link_b + kb + gb)
        mb = kb * invb
        hb = link_b * invb
        inv_ref[j] = invb
        m_ref[j] = mb
        h_ref[j] = hb
        return (link_a * m, g * m, g_l + g * h, link_b * mb, gb * mb, g_r + gb * hb)

    link_a, in_a, g_l, link_b, in_b, g_r = lax.fori_loop(
        0, 15, step, (first_link, zero, zero, cond[30], zero, zero), unroll=True
    )
    g = excess[15] + in_a + in_b
    inv = 1.0 / (link_a + link_b + g)
    ha = link_a * inv
    hb = link_b * inv
    inv_ref[15] = inv
    h_ref[15] = ha
    m_ref[15] = hb
    low = link_a * hb
    g_l = g_l + ha * g
    g_r = g_r + hb * g
    ground = excess[31] + g_r + roll_l(g_l, -16)
    up = roll_l(low, -16)
    factors = []
    for s in (16, 32, 64):
        inv = 1.0 / (low + up + ground)
        alpha = low * roll_l(inv, s)
        beta = up * roll_l(inv, -s)
        ground, low, up = (
            ground + alpha * roll_l(ground, s) + beta * roll_l(ground, -s),
            alpha * roll_l(low, s),
            beta * roll_l(up, -s),
        )
        factors.append((alpha, beta))
    (a1, b1), (a2, b2), (a4, b4) = factors
    one = jnp.ones_like(low)
    sums = [
        one,
        a1 + a2 * roll_l(b1, 32),
        a2,
        a2 * roll_l(a1, 32),
        jnp.zeros_like(low),
        b2 * roll_l(b1, -32),
        b2,
        b1 + b2 * roll_l(a1, -32),
    ]
    half = a4 + b4
    inv = 1.0 / ground
    own = [inv * (sums[k] + half * roll_l(sums[(k + 4) % 8], 64)) for k in range(8)]
    before = [roll_l(own[(k + 7) % 8], 16) for k in range(8)]
    return own, before


def total(terms):
    while len(terms) > 1:
        terms = [a + b for a, b in zip(terms[::2], terms[1::2])]
    return terms[0]


def line_solve(rhs, factors, inv_ref, m_ref, h_ref, b_ref, x_ref):
    own, before = factors
    zero = jnp.zeros_like(own[0])

    def forward(i, carry):
        in_a, b_l, in_b, b_r = carry
        j = 30 - i
        b = rhs[i] + in_a
        bb = rhs[j] + in_b
        b_ref[i] = b
        b_ref[j] = bb
        return (m_ref[i] * b, b_l + h_ref[i] * b, m_ref[j] * bb, b_r + h_ref[j] * bb)

    in_a, b_l, in_b, b_r = lax.fori_loop(0, 15, forward, (zero, zero, zero, zero), unroll=True)
    mid = rhs[15] + in_a + in_b
    b_l = b_l + h_ref[15] * mid
    b_r = b_r + m_ref[15] * mid
    b = rhs[31] + b_r
    turns = [roll_l(b, 16 * k) + roll_l(b_l, 16 * k - 16) for k in range(8)]
    x_r = total([f * t for f, t in zip(own, turns)])
    x_l = total([f * t for f, t in zip(before, turns)])
    x_ref[31] = x_r
    mid = inv_ref[15] * mid + h_ref[15] * x_l + m_ref[15] * x_r
    x_ref[15] = mid

    def backward(n, carry):
        x_a, x_b = carry
        i = 14 - n
        j = 16 + n
        x_a = m_ref[i] * x_a + (inv_ref[i] * b_ref[i] + h_ref[i] * x_l)
        x_b = m_ref[j] * x_b + (inv_ref[j] * b_ref[j] + h_ref[j] * x_r)
        x_ref[i] = x_a
        x_ref[j] = x_b
        return (x_a, x_b)

    lax.fori_loop(0, 15, backward, (mid, mid), unroll=True)


def kernel(
    v_hbm, imp_hbm, mat_hbm, o_ref,
    v_ref, imp_ref, mat_ref, in_sem, pack, recv, send_back, got_back, grid,
    cond, excess, rhs0, rhs1, fx, fy, ccond, cexcess, inv, m, h, cinv, cm, ch, bb, x0, x1, xc, crhs, cbb,
    main_send, edge_send, inner_send, arrived, fwd_send, fwd_recv, back_send, back_recv,
):
    gy, gz = lax.axis_index("gy"), lax.axis_index("gz")
    core = lax.rem(gy, 2)
    number = (TILES * gz + 15) // 16
    owner = (number < OWNERS) & (owner_place(number) == gz)
    par, tile = lax.rem(number, 2), lax.rem(number // 2, TILES)
    chip = gy - core
    strip = chip + par
    edge_from = lax.rem(strip + GYS - 1 + 2 * core, GYS)

    fetch = [
        pltpu.make_async_copy(v_hbm, v_ref, in_sem.at[0]),
        pltpu.make_async_copy(mat_hbm, mat_ref, in_sem.at[1]),
        pltpu.make_async_copy(imp_hbm, imp_ref, in_sem.at[2]),
    ]
    for copy in fetch:
        copy.start()

    def hello(*device):
        pl.semaphore_signal(barrier, 1, device_id=device, device_id_type=MESH)

    barrier = pltpu.get_barrier_semaphore()

    @pl.when(owner)
    def _():
        for k in FAR_FIRST:
            other = lax.rem(gz + k, SEGS)
            if k:
                hello(strip, other)
                hello(edge_from, other)
            else:

                @pl.when(strip != gy)
                def _():
                    hello(strip, other)

                @pl.when(edge_from != gy)
                def _():
                    hello(edge_from, other)

                hello(chip + 1 - core, gz)

    lane = lax.broadcasted_iota(jnp.int32, (16, 128), 1)
    row = lax.broadcasted_iota(jnp.int32, (16, 128), 0)
    blk = lane // 16
    win = lax.rem(lane, 16)

    for copy in fetch:
        copy.wait()

    def pack_field(a):
        planes = []
        for z in range(8):
            v = v_ref[z]
            mat = mat_ref[z]
            if a == 0:
                f = v
            elif a == 1:
                f = jnp.where(mat == 0, 1.0, jnp.where(mat == 1, 0.33, 0.64)).astype(F32)
            else:
                charge = 0.5 * imp_ref[z].astype(F32) - 1.5
                f = jnp.where(mat == 0, jnp.exp(v) - jnp.exp(-v) - charge, 0.0)
            planes.append(f)
        for j in range(TILES):
            out = roll_l(planes[7], 16 * 7 - WIDE * j + 3)
            for z in range(7):
                out = jnp.where(blk == z, roll_l(planes[z], 16 * z - WIDE * j + 3), out)
            pack[j, a] = out

    for a in range(3):
        pack_field(a)

    pl.semaphore_wait(barrier, 4 * TILES)

    def copy_of(part, j, rows, device, send, got):
        a, n = FIELDS[part]
        src, dst, count = rows
        return pltpu.make_async_remote_copy(
            src_ref=pack.at[j, pl.ds(a, n), pl.ds(src, count)],
            dst_ref=recv.at[gz // 4, lax.rem(gz, 4), pl.ds(a, n), pl.ds(dst, count)],
            send_sem=send,
            recv_sem=got,
            device_id=device,
            device_id_type=MESH,
        )

    def main_copy(part, k, to_core):
        j = lax.rem(tile + k, TILES)
        return copy_of(
            part, j, MAIN[part][to_core], (chip + to_core, owner_place(2 * j + core)),
            main_send.at[part, to_core, k], arrived.at[part, lax.rem(gz, 4)],
        )

    def inner_copy(k):
        j = lax.rem(tile + k, TILES)
        return copy_of(
            1, j, INNER, (chip + 1, owner_place(2 * j + core)),
            inner_send.at[k], arrived.at[1, lax.rem(gz, 4)],
        )

    def edge_copy(part, k, upper):
        j = lax.rem(tile + k, TILES)
        to = lax.rem(gy + core + (GYS - 1 if upper else 0), GYS)
        return copy_of(
            part, j, (UPPER if upper else LOWER)[part], (to, owner_place(2 * j + 1 - core)),
            edge_send.at[part, upper, k], arrived.at[part, lax.rem(gz, 4)],
        )

    def keep(part, rows):
        a, n = FIELDS[part]
        src, dst, count = rows
        pltpu.make_async_copy(
            pack.at[tile, pl.ds(a, n), pl.ds(src, count)],
            recv.at[gz // 4, lax.rem(gz, 4), pl.ds(a, n), pl.ds(dst, count)],
            arrived.at[part, lax.rem(gz, 4)],
        ).start()

    main_self = [owner & (par == core) & (core == to_core) for to_core in (0, 1)]
    edge_self = [owner & (core == 0) & (par == 1), owner & (core == 1) & (par == 0)]

    def start_all(part):
        for k in TILES_FAR_FIRST:
            for w in (0, 1):
                if k:
                    main_copy(part, k, w).start()
                    edge_copy(part, k, w).start()
                    if part and w:
                        inner_copy(k).start()
                else:

                    @pl.when(main_self[w])
                    def _():
                        keep(part, MAIN[part][w])
                        if part and w:
                            keep(part, INNER)

                    @pl.when(jnp.logical_not(main_self[w]))
                    def _():
                        main_copy(part, k, w).start()
                        if part and w:
                            inner_copy(k).start()

                    @pl.when(edge_self[w])
                    def _():
                        keep(part, (UPPER if w else LOWER)[part])

                    @pl.when(jnp.logical_not(edge_self[w]))
                    def _():
                        edge_copy(part, k, w).start()

    def sent_all(part):
        for k in range(TILES):
            for w in (0, 1):
                if k:
                    main_copy(part, k, w).wait_send()
                    edge_copy(part, k, w).wait_send()
                    if part and w:
                        inner_copy(k).wait_send()
                else:

                    @pl.when(jnp.logical_not(main_self[w]))
                    def _():
                        main_copy(part, k, w).wait_send()
                        if part and w:
                            inner_copy(k).wait_send()

                    @pl.when(jnp.logical_not(edge_self[w]))
                    def _():
                        edge_copy(part, k, w).wait_send()

    slot = core * TILES + tile

    def back_copy(to):
        return pltpu.make_async_remote_copy(
            src_ref=send_back.at[to],
            dst_ref=got_back.at[slot],
            send_sem=back_send.at[to],
            recv_sem=back_recv.at[core],
            device_id=(strip, to),
            device_id_type=MESH,
        )

    start_all(0)
    sent_all(0)
    start_all(1)

    @pl.when(owner)
    def _():
        y = strip * 16 + core * 8 + jnp.where(row < 12, row, row - 16)
        x = tile * WIDE - 3 + win
        inside = ((row <= 10) | (row >= 13)) & (y >= 0) & (y < GYS * 16) & (x >= 0) & (x < 128)
        odd_cell = lax.rem(row + win, 2) == 1
        inner = inside & ((row <= 9) | (row >= 14))
        colour0 = inner & odd_cell
        colour1 = inner & jnp.logical_not(odd_cell)

        def forward_copy(q, frm):
            src, dst, count = FORWARD[frm]
            return pltpu.make_async_remote_copy(
                src_ref=recv.at[:, q, pl.ds(0, 2), pl.ds(src, count)],
                dst_ref=recv.at[:, q, pl.ds(0, 2), pl.ds(dst, count)],
                send_sem=fwd_send.at[q],
                recv_sem=fwd_recv.at[q],
                device_id=(chip + 1 - frm, gz),
                device_id_type=MESH,
            )

        def landed(part, q):
            a, n = FIELDS[part]
            piece = recv.at[:, q, pl.ds(a, n), pl.ds(0, ROWS[part])]
            pltpu.make_async_copy(piece, piece, arrived.at[part, q]).wait()

        for q in range(4):
            landed(0, q)
            for frm in (0, 1):

                @pl.when(core == frm)
                def _():
                    forward_copy(q, frm).start()

        for q in range(4):
            piece = recv.at[:, q, pl.ds(0, 2), pl.ds(0, 3)]
            pltpu.make_async_copy(piece, piece, fwd_recv.at[q]).wait()
            for a in range(2):
                parts = swap_blocks([recv[c, q, a] for c in range(8)], blk)
                for z in range(8):
                    grid[a, 8 * q + z] = jnp.where(inside, parts[z], 0.0)

        for a in range(2):
            grid[a, 32] = jnp.where(blk == 7, 0.0, roll_l(grid[a, 0], -16))

        k_last = ZW * face(grid[1, 31], grid[1, 32])
        flow_last = k_last * (grid[0, 32] - grid[0, 31])
        k_floor = ZW * grid[1, 0]
        at_floor = blk == 0
        first_link = jnp.where(at_floor, 0.0, roll_l(k_last, 16))
        flow_first = jnp.where(at_floor, k_floor * grid[0, 0], roll_l(flow_last, 16))
        outside_one = jnp.where(inside, 0.0, 1.0)

        def quad(f):
            f = f + roll_l(f, -1)
            return f + pltpu.roll(f, 7, 0)

        def assemble(i, flow_below):
            v = grid[0, i]
            p = grid[1, i]
            kz = ZW * face(p, grid[1, i + 1])
            flow = kz * (grid[0, i + 1] - v)
            px = face(p, roll_l(p, -1))
            py = face(p, roll_r(p, -1))
            flow_x = px * (roll_l(v, -1) - v)
            flow_y = py * (roll_r(v, -1) - v)
            soft = jnp.where(p == 1.0, jnp.exp(v) + jnp.exp(-v), 0.0) + outside_one
            extra = (px + roll_l(px, 1)) + (py + roll_r(py, 1)) + soft
            rhs0[i] = (flow - flow_below) + (flow_x - roll_l(flow_x, 1)) + (flow_y - roll_r(flow_y, 1))
            cond[i] = kz
            excess[i] = extra
            fx[i] = px
            fy[i] = py
            ccond[i] = quad(kz[:8])
            e2 = extra[:8] + roll_l(extra[:8], -1) - 2.0 * px[:8]
            y2 = py[:8] + roll_l(py[:8], -1)
            cexcess[i] = e2 + pltpu.roll(e2, 7, 0) - 2.0 * y2
            return flow

        lax.fori_loop(0, 32, assemble, flow_first, unroll=32)

        floor = jnp.where(at_floor, k_floor, 0.0)
        roof = jnp.where(blk == 7, k_last, 0.0)
        excess[0] = excess[0] + floor
        excess[31] = excess[31] + roof
        cexcess[0] = cexcess[0] + quad(floor[:8])
        cexcess[31] = cexcess[31] + quad(roof[:8])

        fine = eliminate(cond, excess, first_link, inv, m, h, blk)
        coarse = eliminate(ccond, cexcess, quad(first_link[:8]), cinv, cm, ch, blk)

        for q in range(4):
            landed(1, q)
            parts = swap_blocks([recv[c, q, 2] for c in range(8)], blk)
            for z in range(8):
                force = rhs0[8 * q + z] - parts[z]
                rhs0[8 * q + z] = jnp.where(colour0, force, 0.0)
                rhs1[8 * q + z] = jnp.where(colour1, force, 0.0)

        line_solve(rhs0, fine, inv, m, h, bb, x0)

        def lateral(f, i):
            gx, gyy = fx[i], fy[i]
            return (gx * roll_l(f, -1) + roll_l(gx * f, 1)) + (gyy * roll_r(f, -1) + roll_r(gyy * f, 1))

        def side(i, carry):
            rhs1[i] = jnp.where(colour1, rhs1[i] + lateral(x0[i], i), 0.0)
            return carry

        lax.fori_loop(0, 32, side, 0, unroll=32)
        line_solve(rhs1, fine, inv, m, h, bb, x1)

        def restrict(i, carry):
            f = x1[i]
            g = fy[i] * f
            gx, gyy, t = fx[i, :8], fy[i, :8], f[:8]
            out = (gx * roll_l(t, -1) + roll_l(gx * t, 1)) + (
                gyy * roll_r(f, -1)[:8] + roll_r(g, 1)[:8]
            )
            crhs[i] = quad(jnp.where(colour0[:8], out, 0.0))
            return carry

        lax.fori_loop(0, 32, restrict, 0, unroll=32)
        line_solve(crhs, coarse, cinv, cm, ch, cbb, xc)

        odd_x = lax.rem(lane, 2) == 1
        even_y = lax.rem(row, 2) == 0

        for q in range(4):
            parts = []
            for z in range(8):
                i = 8 * q + z
                f = xc[i]
                f = jnp.where(odd_x[:8], f, roll_l(f, 1))
                f = jnp.where(even_y[:8], f, pltpu.roll(f, 1, 0))
                parts.append(x0[i, :8] + x1[i, :8] + f)
            for c, f in enumerate(swap_blocks(parts, blk[:8])):
                send_back[4 * c + q] = f


        for k in FAR_FIRST:
            to = lax.rem(gz + k, SEGS)
            if k:
                back_copy(to).start()
            else:

                @pl.when(strip == gy)
                def _():
                    pltpu.make_async_copy(
                        send_back.at[gz], got_back.at[slot], back_recv.at[core]
                    ).start()

                @pl.when(strip != gy)
                def _():
                    back_copy(to).start()

        for q in range(4):
            for frm in (0, 1):

                @pl.when(core == frm)
                def _():
                    forward_copy(q, frm).wait_send()

    sent_all(1)


    column = lane[:8] // WIDE
    for to_core in (0, 1):
        rows = pl.ds(8 * to_core, 8)
        piece = got_back.at[pl.ds(to_core * TILES, TILES)]
        pltpu.make_async_copy(piece, piece, back_recv.at[to_core]).wait()
        for z in range(8):
            f = roll_l(got_back[to_core * TILES], -3 - 16 * z)
            for j in range(1, TILES):
                f = jnp.where(
                    column == j, roll_l(got_back[to_core * TILES + j], WIDE * j - 3 - 16 * z), f
                )
            o_ref[z, rows] = v_ref[z, rows] + f

    @pl.when(owner)
    def _():
        for k in range(SEGS):
            if k:
                back_copy(lax.rem(gz + k, SEGS)).wait_send()
            else:

                @pl.when(strip != gy)
                def _():
                    back_copy(gz).wait_send()


def body(electric_level, impurity_atoms, cell_materials):
    fields = (electric_level, impurity_atoms, cell_materials)
    line = pltpu.VMEM((32, 16, 128), F32)
    half = pltpu.VMEM((32, 8, 128), F32)
    vmem = pl.BlockSpec(memory_space=pltpu.VMEM)
    return pl.pallas_call(
        kernel,
        out_shape=jax.ShapeDtypeStruct(electric_level.shape, F32),
        in_specs=[pl.BlockSpec(memory_space=pltpu.HBM)] * 3,
        out_specs=vmem,
        scratch_shapes=[
            pltpu.VMEM(electric_level.shape, F32),
            pltpu.VMEM(electric_level.shape, jnp.int32),
            pltpu.VMEM(electric_level.shape, jnp.int32),
            pltpu.SemaphoreType.DMA((3,)),
            pltpu.VMEM((TILES, 3, 16, 128), F32),
            pltpu.VMEM((8, 4, 3, 16, 128), F32),
            pltpu.VMEM((SEGS, 8, 128), F32),
            pltpu.VMEM((OWNERS, 8, 128), F32),
            pltpu.VMEM((2, 33, 16, 128), F32),
        ]
        + [line] * 6
        + [half] * 2
        + [line] * 3
        + [half] * 3
        + [line] * 3
        + [half] * 3
        + [pltpu.SemaphoreType.DMA((2, 2, TILES))] * 2
        + [pltpu.SemaphoreType.DMA((TILES,)), pltpu.SemaphoreType.DMA((2, 4))]
        + [pltpu.SemaphoreType.DMA((4,))] * 2
        + [pltpu.SemaphoreType.DMA((SEGS,)), pltpu.SemaphoreType.DMA((2,))],
        compiler_params=pltpu.CompilerParams(
            collective_id=0, has_side_effects=True, vmem_limit_bytes=32 * 1024 * 1024
        ),
        cost_estimate=pl.CostEstimate(flops=20_000_000, bytes_accessed=262144, transcendentals=200_000),
        name="newton_step",
    )(*(pltpu.with_memory_space_constraint(f, pltpu.HBM) for f in fields))


def solution(mesh):
    placed = P("gz", "gy", None)
    return jax.shard_map(
        body, mesh=mesh, in_specs=(placed,) * 3, out_specs=placed, check_vma=False
    )
```

```python
import jax
import jax.numpy as jnp
from jax import lax
from jax.experimental import pallas as pl
from jax.experimental.pallas import tpu as pltpu
from jax.sharding import PartitionSpec as P

MESH = pl.DeviceIdType.MESH
ZW = 8192.0
SEGS = 32
GYS = 16
F32 = jnp.float32


def hops(k):
    x, z = k // 8, k % 8
    return min(x, 4 - x) + min(z, 8 - z)


FAR_FIRST = sorted(range(SEGS), key=lambda k: -hops(k))
WIDE = 10
TILES = 13
OWNERS = 2 * TILES
TILES_FAR_FIRST = sorted(range(TILES), key=lambda k: -hops((SEGS * k // TILES) % SEGS))


def owner_place(n):
    return 8 * (n % 4) + n // 4


def roll_l(v, s):
    return pltpu.roll(v, s % 128, 1) if s % 128 else v


def roll_r(v, s):
    return pltpu.roll(v, s % 16, 0)


def swap_blocks(rows, blk):
    rows = list(rows)
    for bit in (1, 2, 4):
        keep = (blk & bit) == 0
        for i in range(8):
            if not i & bit:
                a, c = rows[i], rows[i | bit]
                rows[i] = jnp.where(keep, a, roll_l(c, 16 * bit))
                rows[i | bit] = jnp.where(keep, roll_l(a, -16 * bit), c)
    return rows


def face(a, b):
    total = a + b
    prod = a * b
    return jnp.where(prod > 0, 2.0 * prod / total, total)


MAIN = (((0, 0, 8), (8, 0, 8)), ((0, 0, 10), (8, 0, 8)))
INNER = (6, 14, 2)
LOWER = ((13, 13, 3), (14, 14, 2))
UPPER = ((0, 8, 3), (0, 8, 2))
FORWARD = ((5, 13, 3), (0, 8, 3))
ROWS = (11, 12)
FIELDS = ((0, 2), (2, 1))


def eliminate(cond, excess, first_link, inv_ref, m_ref, h_ref, blk):
    zero = jnp.zeros_like(first_link)

    def step(i, carry):
        link_a, in_a, g_l, link_b, in_b, g_r = carry
        j = 30 - i
        g = excess[i] + in_a
        k = cond[i]
        inv = 1.0 / (link_a + k + g)
        m = k * inv
        h = link_a * inv
        inv_ref[i] = inv
        m_ref[i] = m
        h_ref[i] = h
        gb = excess[j] + in_b
        kb = cond[j - 1]
        invb = 1.0 / (link_b + kb + gb)
        mb = kb * invb
        hb = link_b * invb
        inv_ref[j] = invb
        m_ref[j] = mb
        h_ref[j] = hb
        return (link_a * m, g * m, g_l + g * h, link_b * mb, gb * mb, g_r + gb * hb)

    link_a, in_a, g_l, link_b, in_b, g_r = lax.fori_loop(
        0, 15, step, (first_link, zero, zero, cond[30], zero, zero), unroll=True
    )
    g = excess[15] + in_a + in_b
    inv = 1.0 / (link_a + link_b + g)
    ha = link_a * inv
    hb = link_b * inv
    inv_ref[15] = inv
    h_ref[15] = ha
    m_ref[15] = hb
    low = link_a * hb
    g_l = g_l + ha * g
    g_r = g_r + hb * g
    ground = excess[31] + g_r + roll_l(g_l, -16)
    up = roll_l(low, -16)
    factors = []
    for s in (16, 32, 64):
        inv = 1.0 / (low + up + ground)
        alpha = low * roll_l(inv, s)
        beta = up * roll_l(inv, -s)
        ground, low, up = (
            ground + alpha * roll_l(ground, s) + beta * roll_l(ground, -s),
            alpha * roll_l(low, s),
            beta * roll_l(up, -s),
        )
        factors.append((alpha, beta))
    (a1, b1), (a2, b2), (a4, b4) = factors
    one = jnp.ones_like(low)
    sums = [
        one,
        a1 + a2 * roll_l(b1, 32),
        a2,
        a2 * roll_l(a1, 32),
        jnp.zeros_like(low),
        b2 * roll_l(b1, -32),
        b2,
        b1 + b2 * roll_l(a1, -32),
    ]
    half = a4 + b4
    inv = 1.0 / ground
    own = [inv * (sums[k] + half * roll_l(sums[(k + 4) % 8], 64)) for k in range(8)]
    before = [roll_l(own[(k + 7) % 8], 16) for k in range(8)]
    return own, before


def total(terms):
    while len(terms) > 1:
        terms = [a + b for a, b in zip(terms[::2], terms[1::2])]
    return terms[0]


def line_solve(rhs, factors, inv_ref, m_ref, h_ref, b_ref, x_ref):
    own, before = factors
    zero = jnp.zeros_like(own[0])

    def forward(i, carry):
        in_a, b_l, in_b, b_r = carry
        j = 30 - i
        b = rhs[i] + in_a
        bb = rhs[j] + in_b
        b_ref[i] = b
        b_ref[j] = bb
        return (m_ref[i] * b, b_l + h_ref[i] * b, m_ref[j] * bb, b_r + h_ref[j] * bb)

    in_a, b_l, in_b, b_r = lax.fori_loop(0, 15, forward, (zero, zero, zero, zero), unroll=True)
    mid = rhs[15] + in_a + in_b
    b_l = b_l + h_ref[15] * mid
    b_r = b_r + m_ref[15] * mid
    b = rhs[31] + b_r
    turns = [roll_l(b, 16 * k) + roll_l(b_l, 16 * k - 16) for k in range(8)]
    x_r = total([f * t for f, t in zip(own, turns)])
    x_l = total([f * t for f, t in zip(before, turns)])
    x_ref[31] = x_r
    mid = inv_ref[15] * mid + h_ref[15] * x_l + m_ref[15] * x_r
    x_ref[15] = mid

    def backward(n, carry):
        x_a, x_b = carry
        i = 14 - n
        j = 16 + n
        x_a = m_ref[i] * x_a + (inv_ref[i] * b_ref[i] + h_ref[i] * x_l)
        x_b = m_ref[j] * x_b + (inv_ref[j] * b_ref[j] + h_ref[j] * x_r)
        x_ref[i] = x_a
        x_ref[j] = x_b
        return (x_a, x_b)

    lax.fori_loop(0, 15, backward, (mid, mid), unroll=True)


def kernel(
    v_hbm, imp_hbm, mat_hbm, o_ref,
    v_ref, imp_ref, mat_ref, in_sem, pack, recv, send_back, got_back, grid,
    cond, excess, rhs0, rhs1, fx, fy, ccond, cexcess, inv, m, h, cinv, cm, ch, bb, x0, x1, xc, crhs, cbb,
    main_send, edge_send, inner_send, arrived, fwd_send, fwd_recv, back_send, back_recv,
):
    gy, gz = lax.axis_index("gy"), lax.axis_index("gz")
    core = lax.rem(gy, 2)
    number = 4 * lax.rem(gz, 8) + gz // 8
    owner = number < OWNERS
    par, tile = lax.rem(number, 2), lax.rem(number // 2, TILES)
    chip = gy - core
    strip = chip + par
    edge_from = lax.rem(strip + GYS - 1 + 2 * core, GYS)

    fetch = [
        pltpu.make_async_copy(v_hbm, v_ref, in_sem.at[0]),
        pltpu.make_async_copy(mat_hbm, mat_ref, in_sem.at[1]),
        pltpu.make_async_copy(imp_hbm, imp_ref, in_sem.at[2]),
    ]
    for copy in fetch:
        copy.start()

    def hello(*device):
        pl.semaphore_signal(barrier, 1, device_id=device, device_id_type=MESH)

    barrier = pltpu.get_barrier_semaphore()

    @pl.when(owner)
    def _():
        for k in FAR_FIRST:
            other = lax.rem(gz + k, SEGS)
            if k:
                hello(strip, other)
                hello(edge_from, other)
            else:

                @pl.when(strip != gy)
                def _():
                    hello(strip, other)

                @pl.when(edge_from != gy)
                def _():
                    hello(edge_from, other)

                hello(chip + 1 - core, gz)

    lane = lax.broadcasted_iota(jnp.int32, (16, 128), 1)
    row = lax.broadcasted_iota(jnp.int32, (16, 128), 0)
    blk = lane // 16
    win = lax.rem(lane, 16)

    for copy in fetch:
        copy.wait()

    def pack_field(a):
        planes = []
        for z in range(8):
            v = v_ref[z]
            mat = mat_ref[z]
            if a == 0:
                f = v
            elif a == 1:
                f = jnp.where(mat == 0, 1.0, jnp.where(mat == 1, 0.33, 0.64)).astype(F32)
            else:
                charge = 0.5 * imp_ref[z].astype(F32) - 1.5
                f = jnp.where(mat == 0, jnp.exp(v) - jnp.exp(-v) - charge, 0.0)
            planes.append(f)
        for j in range(TILES):
            out = roll_l(planes[7], 16 * 7 - WIDE * j + 3)
            for z in range(7):
                out = jnp.where(blk == z, roll_l(planes[z], 16 * z - WIDE * j + 3), out)
            pack[j, a] = out

    for a in range(3):
        pack_field(a)

    pl.semaphore_wait(barrier, 4 * TILES)

    def copy_of(part, j, rows, device, send, got):
        a, n = FIELDS[part]
        src, dst, count = rows
        return pltpu.make_async_remote_copy(
            src_ref=pack.at[j, pl.ds(a, n), pl.ds(src, count)],
            dst_ref=recv.at[gz // 4, lax.rem(gz, 4), pl.ds(a, n), pl.ds(dst, count)],
            send_sem=send,
            recv_sem=got,
            device_id=device,
            device_id_type=MESH,
        )

    def main_copy(part, k, to_core):
        j = lax.rem(tile + k, TILES)
        return copy_of(
            part, j, MAIN[part][to_core], (chip + to_core, owner_place(2 * j + core)),
            main_send.at[part, to_core, k], arrived.at[part, lax.rem(gz, 4)],
        )

    def inner_copy(k):
        j = lax.rem(tile + k, TILES)
        return copy_of(
            1, j, INNER, (chip + 1, owner_place(2 * j + core)),
            inner_send.at[k], arrived.at[1, lax.rem(gz, 4)],
        )

    def edge_copy(part, k, upper):
        j = lax.rem(tile + k, TILES)
        to = lax.rem(gy + core + (GYS - 1 if upper else 0), GYS)
        return copy_of(
            part, j, (UPPER if upper else LOWER)[part], (to, owner_place(2 * j + 1 - core)),
            edge_send.at[part, upper, k], arrived.at[part, lax.rem(gz, 4)],
        )

    def keep(part, rows):
        a, n = FIELDS[part]
        src, dst, count = rows
        pltpu.make_async_copy(
            pack.at[tile, pl.ds(a, n), pl.ds(src, count)],
            recv.at[gz // 4, lax.rem(gz, 4), pl.ds(a, n), pl.ds(dst, count)],
            arrived.at[part, lax.rem(gz, 4)],
        ).start()

    main_self = [owner & (par == core) & (core == to_core) for to_core in (0, 1)]
    edge_self = [owner & (core == 0) & (par == 1), owner & (core == 1) & (par == 0)]

    def start_all(part):
        for k in TILES_FAR_FIRST:
            for w in (0, 1):
                if k:
                    main_copy(part, k, w).start()
                    edge_copy(part, k, w).start()
                    if part and w:
                        inner_copy(k).start()
                else:

                    @pl.when(main_self[w])
                    def _():
                        keep(part, MAIN[part][w])
                        if part and w:
                            keep(part, INNER)

                    @pl.when(jnp.logical_not(main_self[w]))
                    def _():
                        main_copy(part, k, w).start()
                        if part and w:
                            inner_copy(k).start()

                    @pl.when(edge_self[w])
                    def _():
                        keep(part, (UPPER if w else LOWER)[part])

                    @pl.when(jnp.logical_not(edge_self[w]))
                    def _():
                        edge_copy(part, k, w).start()

    def sent_all(part):
        for k in range(TILES):
            for w in (0, 1):
                if k:
                    main_copy(part, k, w).wait_send()
                    edge_copy(part, k, w).wait_send()
                    if part and w:
                        inner_copy(k).wait_send()
                else:

                    @pl.when(jnp.logical_not(main_self[w]))
                    def _():
                        main_copy(part, k, w).wait_send()
                        if part and w:
                            inner_copy(k).wait_send()

                    @pl.when(jnp.logical_not(edge_self[w]))
                    def _():
                        edge_copy(part, k, w).wait_send()

    slot = core * TILES + tile

    def back_copy(to):
        return pltpu.make_async_remote_copy(
            src_ref=send_back.at[to],
            dst_ref=got_back.at[slot],
            send_sem=back_send.at[to],
            recv_sem=back_recv.at[core],
            device_id=(strip, to),
            device_id_type=MESH,
        )

    start_all(0)
    sent_all(0)
    start_all(1)

    @pl.when(owner)
    def _():
        y = strip * 16 + core * 8 + jnp.where(row < 12, row, row - 16)
        x = tile * WIDE - 3 + win
        inside = ((row <= 10) | (row >= 13)) & (y >= 0) & (y < GYS * 16) & (x >= 0) & (x < 128)
        odd_cell = lax.rem(row + win, 2) == 1
        inner = inside & ((row <= 9) | (row >= 14))
        colour0 = inner & odd_cell
        colour1 = inner & jnp.logical_not(odd_cell)

        def forward_copy(q, frm):
            src, dst, count = FORWARD[frm]
            return pltpu.make_async_remote_copy(
                src_ref=recv.at[:, q, pl.ds(0, 2), pl.ds(src, count)],
                dst_ref=recv.at[:, q, pl.ds(0, 2), pl.ds(dst, count)],
                send_sem=fwd_send.at[q],
                recv_sem=fwd_recv.at[q],
                device_id=(chip + 1 - frm, gz),
                device_id_type=MESH,
            )

        def landed(part, q):
            a, n = FIELDS[part]
            piece = recv.at[:, q, pl.ds(a, n), pl.ds(0, ROWS[part])]
            pltpu.make_async_copy(piece, piece, arrived.at[part, q]).wait()

        for q in range(4):
            landed(0, q)
            for frm in (0, 1):

                @pl.when(core == frm)
                def _():
                    forward_copy(q, frm).start()

        for q in range(4):
            piece = recv.at[:, q, pl.ds(0, 2), pl.ds(0, 3)]
            pltpu.make_async_copy(piece, piece, fwd_recv.at[q]).wait()
            for a in range(2):
                parts = swap_blocks([recv[c, q, a] for c in range(8)], blk)
                for z in range(8):
                    grid[a, 8 * q + z] = jnp.where(inside, parts[z], 0.0)

        for a in range(2):
            grid[a, 32] = jnp.where(blk == 7, 0.0, roll_l(grid[a, 0], -16))

        k_last = ZW * face(grid[1, 31], grid[1, 32])
        flow_last = k_last * (grid[0, 32] - grid[0, 31])
        k_floor = ZW * grid[1, 0]
        at_floor = blk == 0
        first_link = jnp.where(at_floor, 0.0, roll_l(k_last, 16))
        flow_first = jnp.where(at_floor, k_floor * grid[0, 0], roll_l(flow_last, 16))
        outside_one = jnp.where(inside, 0.0, 1.0)

        def quad(f):
            f = f + roll_l(f, -1)
            return f + pltpu.roll(f, 7, 0)

        def assemble(i, flow_below):
            v = grid[0, i]
            p = grid[1, i]
            kz = ZW * face(p, grid[1, i + 1])
            flow = kz * (grid[0, i + 1] - v)
            px = face(p, roll_l(p, -1))
            py = face(p, roll_r(p, -1))
            flow_x = px * (roll_l(v, -1) - v)
            flow_y = py * (roll_r(v, -1) - v)
            soft = jnp.where(p == 1.0, jnp.exp(v) + jnp.exp(-v), 0.0) + outside_one
            extra = (px + roll_l(px, 1)) + (py + roll_r(py, 1)) + soft
            rhs0[i] = (flow - flow_below) + (flow_x - roll_l(flow_x, 1)) + (flow_y - roll_r(flow_y, 1))
            cond[i] = kz
            excess[i] = extra
            fx[i] = px
            fy[i] = py
            ccond[i] = quad(kz[:8])
            e2 = extra[:8] + roll_l(extra[:8], -1) - 2.0 * px[:8]
            y2 = py[:8] + roll_l(py[:8], -1)
            cexcess[i] = e2 + pltpu.roll(e2, 7, 0) - 2.0 * y2
            return flow

        lax.fori_loop(0, 32, assemble, flow_first, unroll=32)

        floor = jnp.where(at_floor, k_floor, 0.0)
        roof = jnp.where(blk == 7, k_last, 0.0)
        excess[0] = excess[0] + floor
        excess[31] = excess[31] + roof
        cexcess[0] = cexcess[0] + quad(floor[:8])
        cexcess[31] = cexcess[31] + quad(roof[:8])

        fine = eliminate(cond, excess, first_link, inv, m, h, blk)
        coarse = eliminate(ccond, cexcess, quad(first_link[:8]), cinv, cm, ch, blk)

        for q in range(4):
            landed(1, q)
            parts = swap_blocks([recv[c, q, 2] for c in range(8)], blk)
            for z in range(8):
                force = rhs0[8 * q + z] - parts[z]
                rhs0[8 * q + z] = jnp.where(colour0, force, 0.0)
                rhs1[8 * q + z] = jnp.where(colour1, force, 0.0)

        line_solve(rhs0, fine, inv, m, h, bb, x0)

        def lateral(f, i):
            gx, gyy = fx[i], fy[i]
            return (gx * roll_l(f, -1) + roll_l(gx * f, 1)) + (gyy * roll_r(f, -1) + roll_r(gyy * f, 1))

        def side(i, carry):
            rhs1[i] = jnp.where(colour1, rhs1[i] + lateral(x0[i], i), 0.0)
            return carry

        lax.fori_loop(0, 32, side, 0, unroll=32)
        line_solve(rhs1, fine, inv, m, h, bb, x1)

        def restrict(i, carry):
            f = x1[i]
            g = fy[i] * f
            gx, gyy, t = fx[i, :8], fy[i, :8], f[:8]
            out = (gx * roll_l(t, -1) + roll_l(gx * t, 1)) + (
                gyy * roll_r(f, -1)[:8] + roll_r(g, 1)[:8]
            )
            crhs[i] = quad(jnp.where(colour0[:8], out, 0.0))
            return carry

        lax.fori_loop(0, 32, restrict, 0, unroll=32)
        line_solve(crhs, coarse, cinv, cm, ch, cbb, xc)

        odd_x = lax.rem(lane, 2) == 1
        even_y = lax.rem(row, 2) == 0

        for q in range(4):
            parts = []
            for z in range(8):
                i = 8 * q + z
                f = xc[i]
                f = jnp.where(odd_x[:8], f, roll_l(f, 1))
                f = jnp.where(even_y[:8], f, pltpu.roll(f, 1, 0))
                parts.append(x0[i, :8] + x1[i, :8] + f)
            for c, f in enumerate(swap_blocks(parts, blk[:8])):
                send_back[4 * c + q] = f


        for k in FAR_FIRST:
            to = lax.rem(gz + k, SEGS)
            if k:
                back_copy(to).start()
            else:

                @pl.when(strip == gy)
                def _():
                    pltpu.make_async_copy(
                        send_back.at[gz], got_back.at[slot], back_recv.at[core]
                    ).start()

                @pl.when(strip != gy)
                def _():
                    back_copy(to).start()

        for q in range(4):
            for frm in (0, 1):

                @pl.when(core == frm)
                def _():
                    forward_copy(q, frm).wait_send()

    sent_all(1)


    column = lane[:8] // WIDE
    for to_core in (0, 1):
        rows = pl.ds(8 * to_core, 8)
        piece = got_back.at[pl.ds(to_core * TILES, TILES)]
        pltpu.make_async_copy(piece, piece, back_recv.at[to_core]).wait()
        for z in range(8):
            f = roll_l(got_back[to_core * TILES], -3 - 16 * z)
            for j in range(1, TILES):
                f = jnp.where(
                    column == j, roll_l(got_back[to_core * TILES + j], WIDE * j - 3 - 16 * z), f
                )
            o_ref[z, rows] = v_ref[z, rows] + f

    @pl.when(owner)
    def _():
        for k in range(SEGS):
            if k:
                back_copy(lax.rem(gz + k, SEGS)).wait_send()
            else:

                @pl.when(strip != gy)
                def _():
                    back_copy(gz).wait_send()


def body(electric_level, impurity_atoms, cell_materials):
    fields = (electric_level, impurity_atoms, cell_materials)
    line = pltpu.VMEM((32, 16, 128), F32)
    half = pltpu.VMEM((32, 8, 128), F32)
    vmem = pl.BlockSpec(memory_space=pltpu.VMEM)
    return pl.pallas_call(
        kernel,
        out_shape=jax.ShapeDtypeStruct(electric_level.shape, F32),
        in_specs=[pl.BlockSpec(memory_space=pltpu.HBM)] * 3,
        out_specs=vmem,
        scratch_shapes=[
            pltpu.VMEM(electric_level.shape, F32),
            pltpu.VMEM(electric_level.shape, jnp.int32),
            pltpu.VMEM(electric_level.shape, jnp.int32),
            pltpu.SemaphoreType.DMA((3,)),
            pltpu.VMEM((TILES, 3, 16, 128), F32),
            pltpu.VMEM((8, 4, 3, 16, 128), F32),
            pltpu.VMEM((SEGS, 8, 128), F32),
            pltpu.VMEM((OWNERS, 8, 128), F32),
            pltpu.VMEM((2, 33, 16, 128), F32),
        ]
        + [line] * 6
        + [half] * 2
        + [line] * 3
        + [half] * 3
        + [line] * 3
        + [half] * 3
        + [pltpu.SemaphoreType.DMA((2, 2, TILES))] * 2
        + [pltpu.SemaphoreType.DMA((TILES,)), pltpu.SemaphoreType.DMA((2, 4))]
        + [pltpu.SemaphoreType.DMA((4,))] * 2
        + [pltpu.SemaphoreType.DMA((SEGS,)), pltpu.SemaphoreType.DMA((2,))],
        compiler_params=pltpu.CompilerParams(
            collective_id=0, has_side_effects=True, vmem_limit_bytes=32 * 1024 * 1024
        ),
        cost_estimate=pl.CostEstimate(flops=20_000_000, bytes_accessed=262144, transcendentals=200_000),
        name="newton_step",
    )(*(pltpu.with_memory_space_constraint(f, pltpu.HBM) for f in fields))


def solution(mesh):
    placed = P("gz", "gy", None)
    return jax.shard_map(
        body, mesh=mesh, in_specs=(placed,) * 3, out_specs=placed, check_vma=False
    )
```

```python
import jax
import jax.numpy as jnp
from jax import lax
from jax.experimental import pallas as pl
from jax.experimental.pallas import tpu as pltpu
from jax.sharding import PartitionSpec as P

MESH = pl.DeviceIdType.MESH
ZW = 8192.0
SEGS = 32
GYS = 16
F32 = jnp.float32


def hops(k):
    x, z = k // 8, k % 8
    return min(x, 4 - x) + min(z, 8 - z)


FAR_FIRST = sorted(range(SEGS), key=lambda k: -hops(k))
WIDE = 10
TILES = 13
OWNERS = 2 * TILES
TILES_FAR_FIRST = sorted(range(TILES), key=lambda k: -hops(16 * (k % 2) + k // 2))


def owner_place(n):
    return 8 * (n % 4) + n // 4


def roll_l(v, s):
    return pltpu.roll(v, s % 128, 1) if s % 128 else v


def roll_r(v, s):
    return pltpu.roll(v, s % 16, 0)


def swap_blocks(rows, blk):
    rows = list(rows)
    for bit in (1, 2, 4):
        keep = (blk & bit) == 0
        for i in range(8):
            if not i & bit:
                a, c = rows[i], rows[i | bit]
                rows[i] = jnp.where(keep, a, roll_l(c, 16 * bit))
                rows[i | bit] = jnp.where(keep, roll_l(a, -16 * bit), c)
    return rows


def face(a, b):
    total = a + b
    prod = a * b
    return jnp.where(prod > 0, 2.0 * prod / total, total)


MAIN = (((0, 0, 8), (8, 0, 8)), ((0, 0, 10), (8, 0, 8)))
INNER = (6, 14, 2)
LOWER = ((13, 13, 3), (14, 14, 2))
UPPER = ((0, 8, 3), (0, 8, 2))
FORWARD = ((5, 13, 3), (0, 8, 3))
ROWS = (11, 12)
FIELDS = ((0, 2), (2, 1))


def eliminate(cond, excess, first_link, inv_ref, m_ref, h_ref, blk):
    zero = jnp.zeros_like(first_link)

    def step(i, carry):
        link_a, in_a, g_l, link_b, in_b, g_r = carry
        j = 30 - i
        g = excess[i] + in_a
        k = cond[i]
        inv = 1.0 / (link_a + k + g)
        m = k * inv
        h = link_a * inv
        inv_ref[i] = inv
        m_ref[i] = m
        h_ref[i] = h
        gb = excess[j] + in_b
        kb = cond[j - 1]
        invb = 1.0 / (link_b + kb + gb)
        mb = kb * invb
        hb = link_b * invb
        inv_ref[j] = invb
        m_ref[j] = mb
        h_ref[j] = hb
        return (link_a * m, g * m, g_l + g * h, link_b * mb, gb * mb, g_r + gb * hb)

    link_a, in_a, g_l, link_b, in_b, g_r = lax.fori_loop(
        0, 15, step, (first_link, zero, zero, cond[30], zero, zero), unroll=True
    )
    g = excess[15] + in_a + in_b
    inv = 1.0 / (link_a + link_b + g)
    ha = link_a * inv
    hb = link_b * inv
    inv_ref[15] = inv
    h_ref[15] = ha
    m_ref[15] = hb
    low = link_a * hb
    g_l = g_l + ha * g
    g_r = g_r + hb * g
    ground = excess[31] + g_r + roll_l(g_l, -16)
    up = roll_l(low, -16)
    factors = []
    for s in (16, 32, 64):
        inv = 1.0 / (low + up + ground)
        alpha = low * roll_l(inv, s)
        beta = up * roll_l(inv, -s)
        ground, low, up = (
            ground + alpha * roll_l(ground, s) + beta * roll_l(ground, -s),
            alpha * roll_l(low, s),
            beta * roll_l(up, -s),
        )
        factors.append((alpha, beta))
    (a1, b1), (a2, b2), (a4, b4) = factors
    one = jnp.ones_like(low)
    sums = [
        one,
        a1 + a2 * roll_l(b1, 32),
        a2,
        a2 * roll_l(a1, 32),
        jnp.zeros_like(low),
        b2 * roll_l(b1, -32),
        b2,
        b1 + b2 * roll_l(a1, -32),
    ]
    half = a4 + b4
    inv = 1.0 / ground
    own = [inv * (sums[k] + half * roll_l(sums[(k + 4) % 8], 64)) for k in range(8)]
    before = [roll_l(own[(k + 7) % 8], 16) for k in range(8)]
    return own, before


def total(terms):
    while len(terms) > 1:
        terms = [a + b for a, b in zip(terms[::2], terms[1::2])]
    return terms[0]


def line_solve(rhs, factors, inv_ref, m_ref, h_ref, b_ref, x_ref):
    own, before = factors
    zero = jnp.zeros_like(own[0])

    def forward(i, carry):
        in_a, b_l, in_b, b_r = carry
        j = 30 - i
        b = rhs[i] + in_a
        bb = rhs[j] + in_b
        b_ref[i] = b
        b_ref[j] = bb
        return (m_ref[i] * b, b_l + h_ref[i] * b, m_ref[j] * bb, b_r + h_ref[j] * bb)

    in_a, b_l, in_b, b_r = lax.fori_loop(0, 15, forward, (zero, zero, zero, zero), unroll=True)
    mid = rhs[15] + in_a + in_b
    b_l = b_l + h_ref[15] * mid
    b_r = b_r + m_ref[15] * mid
    b = rhs[31] + b_r
    turns = [roll_l(b, 16 * k) + roll_l(b_l, 16 * k - 16) for k in range(8)]
    x_r = total([f * t for f, t in zip(own, turns)])
    x_l = total([f * t for f, t in zip(before, turns)])
    x_ref[31] = x_r
    mid = inv_ref[15] * mid + h_ref[15] * x_l + m_ref[15] * x_r
    x_ref[15] = mid

    def backward(n, carry):
        x_a, x_b = carry
        i = 14 - n
        j = 16 + n
        x_a = m_ref[i] * x_a + (inv_ref[i] * b_ref[i] + h_ref[i] * x_l)
        x_b = m_ref[j] * x_b + (inv_ref[j] * b_ref[j] + h_ref[j] * x_r)
        x_ref[i] = x_a
        x_ref[j] = x_b
        return (x_a, x_b)

    lax.fori_loop(0, 15, backward, (mid, mid), unroll=True)


def kernel(
    v_hbm, imp_hbm, mat_hbm, o_ref,
    v_ref, imp_ref, mat_ref, in_sem, pack, recv, send_back, got_back, grid,
    cond, excess, rhs0, rhs1, fx, fy, ccond, cexcess, inv, m, h, cinv, cm, ch, bb, x0, x1, xc, crhs, cbb,
    main_send, edge_send, inner_send, arrived, fwd_send, fwd_recv, back_send, back_recv,
):
    gy, gz = lax.axis_index("gy"), lax.axis_index("gz")
    core = lax.rem(gy, 2)
    number = 4 * lax.rem(gz, 8) + gz // 8
    owner = number < OWNERS
    par, tile = lax.rem(number, 2), lax.rem(number // 2, TILES)
    chip = gy - core
    strip = chip + par
    edge_from = lax.rem(strip + GYS - 1 + 2 * core, GYS)

    fetch = [
        pltpu.make_async_copy(v_hbm, v_ref, in_sem.at[0]),
        pltpu.make_async_copy(mat_hbm, mat_ref, in_sem.at[1]),
        pltpu.make_async_copy(imp_hbm, imp_ref, in_sem.at[2]),
    ]
    for copy in fetch:
        copy.start()

    def hello(*device):
        pl.semaphore_signal(barrier, 1, device_id=device, device_id_type=MESH)

    barrier = pltpu.get_barrier_semaphore()

    @pl.when(owner)
    def _():
        for k in FAR_FIRST:
            other = lax.rem(gz + k, SEGS)
            if k:
                hello(strip, other)
                hello(edge_from, other)
            else:

                @pl.when(strip != gy)
                def _():
                    hello(strip, other)

                @pl.when(edge_from != gy)
                def _():
                    hello(edge_from, other)

                hello(chip + 1 - core, gz)

    lane = lax.broadcasted_iota(jnp.int32, (16, 128), 1)
    row = lax.broadcasted_iota(jnp.int32, (16, 128), 0)
    blk = lane // 16
    win = lax.rem(lane, 16)

    for copy in fetch:
        copy.wait()

    def pack_field(a):
        planes = []
        for z in range(8):
            v = v_ref[z]
            mat = mat_ref[z]
            if a == 0:
                f = v
            elif a == 1:
                f = jnp.where(mat == 0, 1.0, jnp.where(mat == 1, 0.33, 0.64)).astype(F32)
            else:
                charge = 0.5 * imp_ref[z].astype(F32) - 1.5
                f = jnp.where(mat == 0, jnp.exp(v) - jnp.exp(-v) - charge, 0.0)
            planes.append(f)
        for j in range(TILES):
            out = roll_l(planes[7], 16 * 7 - WIDE * j + 3)
            for z in range(7):
                out = jnp.where(blk == z, roll_l(planes[z], 16 * z - WIDE * j + 3), out)
            pack[j, a] = out

    for a in range(3):
        pack_field(a)

    pl.semaphore_wait(barrier, 4 * TILES)

    def copy_of(part, j, rows, device, send, got):
        a, n = FIELDS[part]
        src, dst, count = rows
        return pltpu.make_async_remote_copy(
            src_ref=pack.at[j, pl.ds(a, n), pl.ds(src, count)],
            dst_ref=recv.at[gz // 4, lax.rem(gz, 4), pl.ds(a, n), pl.ds(dst, count)],
            send_sem=send,
            recv_sem=got,
            device_id=device,
            device_id_type=MESH,
        )

    def main_copy(part, k, to_core):
        j = lax.rem(tile + k, TILES)
        return copy_of(
            part, j, MAIN[part][to_core], (chip + to_core, owner_place(2 * j + core)),
            main_send.at[part, to_core, k], arrived.at[part, lax.rem(gz, 4)],
        )

    def inner_copy(k):
        j = lax.rem(tile + k, TILES)
        return copy_of(
            1, j, INNER, (chip + 1, owner_place(2 * j + core)),
            inner_send.at[k], arrived.at[1, lax.rem(gz, 4)],
        )

    def edge_copy(part, k, upper):
        j = lax.rem(tile + k, TILES)
        to = lax.rem(gy + core + (GYS - 1 if upper else 0), GYS)
        return copy_of(
            part, j, (UPPER if upper else LOWER)[part], (to, owner_place(2 * j + 1 - core)),
            edge_send.at[part, upper, k], arrived.at[part, lax.rem(gz, 4)],
        )

    def keep(part, rows):
        a, n = FIELDS[part]
        src, dst, count = rows
        pltpu.make_async_copy(
            pack.at[tile, pl.ds(a, n), pl.ds(src, count)],
            recv.at[gz // 4, lax.rem(gz, 4), pl.ds(a, n), pl.ds(dst, count)],
            arrived.at[part, lax.rem(gz, 4)],
        ).start()

    main_self = [owner & (par == core) & (core == to_core) for to_core in (0, 1)]
    edge_self = [owner & (core == 0) & (par == 1), owner & (core == 1) & (par == 0)]

    def start_all(part):
        for k in TILES_FAR_FIRST:
            for w in (0, 1):
                if k:
                    main_copy(part, k, w).start()
                    edge_copy(part, k, w).start()
                    if part and w:
                        inner_copy(k).start()
                else:

                    @pl.when(main_self[w])
                    def _():
                        keep(part, MAIN[part][w])
                        if part and w:
                            keep(part, INNER)

                    @pl.when(jnp.logical_not(main_self[w]))
                    def _():
                        main_copy(part, k, w).start()
                        if part and w:
                            inner_copy(k).start()

                    @pl.when(edge_self[w])
                    def _():
                        keep(part, (UPPER if w else LOWER)[part])

                    @pl.when(jnp.logical_not(edge_self[w]))
                    def _():
                        edge_copy(part, k, w).start()

    def sent_all(part):
        for k in range(TILES):
            for w in (0, 1):
                if k:
                    main_copy(part, k, w).wait_send()
                    edge_copy(part, k, w).wait_send()
                    if part and w:
                        inner_copy(k).wait_send()
                else:

                    @pl.when(jnp.logical_not(main_self[w]))
                    def _():
                        main_copy(part, k, w).wait_send()
                        if part and w:
                            inner_copy(k).wait_send()

                    @pl.when(jnp.logical_not(edge_self[w]))
                    def _():
                        edge_copy(part, k, w).wait_send()

    slot = core * TILES + tile

    def back_copy(to):
        return pltpu.make_async_remote_copy(
            src_ref=send_back.at[to],
            dst_ref=got_back.at[slot],
            send_sem=back_send.at[to],
            recv_sem=back_recv.at[core],
            device_id=(strip, to),
            device_id_type=MESH,
        )

    start_all(0)
    sent_all(0)
    start_all(1)

    @pl.when(owner)
    def _():
        y = strip * 16 + core * 8 + jnp.where(row < 12, row, row - 16)
        x = tile * WIDE - 3 + win
        inside = ((row <= 10) | (row >= 13)) & (y >= 0) & (y < GYS * 16) & (x >= 0) & (x < 128)
        odd_cell = lax.rem(row + win, 2) == 1
        inner = inside & ((row <= 9) | (row >= 14))
        colour0 = inner & odd_cell
        colour1 = inner & jnp.logical_not(odd_cell)

        def forward_copy(q, frm):
            src, dst, count = FORWARD[frm]
            return pltpu.make_async_remote_copy(
                src_ref=recv.at[:, q, pl.ds(0, 2), pl.ds(src, count)],
                dst_ref=recv.at[:, q, pl.ds(0, 2), pl.ds(dst, count)],
                send_sem=fwd_send.at[q],
                recv_sem=fwd_recv.at[q],
                device_id=(chip + 1 - frm, gz),
                device_id_type=MESH,
            )

        def landed(part, q):
            a, n = FIELDS[part]
            piece = recv.at[:, q, pl.ds(a, n), pl.ds(0, ROWS[part])]
            pltpu.make_async_copy(piece, piece, arrived.at[part, q]).wait()

        for q in range(4):
            landed(0, q)
            for frm in (0, 1):

                @pl.when(core == frm)
                def _():
                    forward_copy(q, frm).start()

        for q in range(4):
            piece = recv.at[:, q, pl.ds(0, 2), pl.ds(0, 3)]
            pltpu.make_async_copy(piece, piece, fwd_recv.at[q]).wait()
            for a in range(2):
                parts = swap_blocks([recv[c, q, a] for c in range(8)], blk)
                for z in range(8):
                    grid[a, 8 * q + z] = jnp.where(inside, parts[z], 0.0)

        for a in range(2):
            grid[a, 32] = jnp.where(blk == 7, 0.0, roll_l(grid[a, 0], -16))

        k_last = ZW * face(grid[1, 31], grid[1, 32])
        flow_last = k_last * (grid[0, 32] - grid[0, 31])
        k_floor = ZW * grid[1, 0]
        at_floor = blk == 0
        first_link = jnp.where(at_floor, 0.0, roll_l(k_last, 16))
        flow_first = jnp.where(at_floor, k_floor * grid[0, 0], roll_l(flow_last, 16))
        outside_one = jnp.where(inside, 0.0, 1.0)

        def quad(f):
            f = f + roll_l(f, -1)
            return f + pltpu.roll(f, 7, 0)

        def assemble(i, flow_below):
            v = grid[0, i]
            p = grid[1, i]
            kz = ZW * face(p, grid[1, i + 1])
            flow = kz * (grid[0, i + 1] - v)
            px = face(p, roll_l(p, -1))
            py = face(p, roll_r(p, -1))
            flow_x = px * (roll_l(v, -1) - v)
            flow_y = py * (roll_r(v, -1) - v)
            soft = jnp.where(p == 1.0, jnp.exp(v) + jnp.exp(-v), 0.0) + outside_one
            extra = (px + roll_l(px, 1)) + (py + roll_r(py, 1)) + soft
            rhs0[i] = (flow - flow_below) + (flow_x - roll_l(flow_x, 1)) + (flow_y - roll_r(flow_y, 1))
            cond[i] = kz
            excess[i] = extra
            fx[i] = px
            fy[i] = py
            ccond[i] = quad(kz[:8])
            e2 = extra[:8] + roll_l(extra[:8], -1) - 2.0 * px[:8]
            y2 = py[:8] + roll_l(py[:8], -1)
            cexcess[i] = e2 + pltpu.roll(e2, 7, 0) - 2.0 * y2
            return flow

        lax.fori_loop(0, 32, assemble, flow_first, unroll=32)

        floor = jnp.where(at_floor, k_floor, 0.0)
        roof = jnp.where(blk == 7, k_last, 0.0)
        excess[0] = excess[0] + floor
        excess[31] = excess[31] + roof
        cexcess[0] = cexcess[0] + quad(floor[:8])
        cexcess[31] = cexcess[31] + quad(roof[:8])

        fine = eliminate(cond, excess, first_link, inv, m, h, blk)
        coarse = eliminate(ccond, cexcess, quad(first_link[:8]), cinv, cm, ch, blk)

        for q in range(4):
            landed(1, q)
            parts = swap_blocks([recv[c, q, 2] for c in range(8)], blk)
            for z in range(8):
                force = rhs0[8 * q + z] - parts[z]
                rhs0[8 * q + z] = jnp.where(colour0, force, 0.0)
                rhs1[8 * q + z] = jnp.where(colour1, force, 0.0)

        line_solve(rhs0, fine, inv, m, h, bb, x0)

        def lateral(f, i):
            gx, gyy = fx[i], fy[i]
            return (gx * roll_l(f, -1) + roll_l(gx * f, 1)) + (gyy * roll_r(f, -1) + roll_r(gyy * f, 1))

        def side(i, carry):
            rhs1[i] = jnp.where(colour1, rhs1[i] + lateral(x0[i], i), 0.0)
            return carry

        lax.fori_loop(0, 32, side, 0, unroll=32)
        line_solve(rhs1, fine, inv, m, h, bb, x1)

        def restrict(i, carry):
            f = x1[i]
            g = fy[i] * f
            gx, gyy, t = fx[i, :8], fy[i, :8], f[:8]
            out = (gx * roll_l(t, -1) + roll_l(gx * t, 1)) + (
                gyy * roll_r(f, -1)[:8] + roll_r(g, 1)[:8]
            )
            crhs[i] = quad(jnp.where(colour0[:8], out, 0.0))
            return carry

        lax.fori_loop(0, 32, restrict, 0, unroll=32)
        line_solve(crhs, coarse, cinv, cm, ch, cbb, xc)

        odd_x = lax.rem(lane, 2) == 1
        even_y = lax.rem(row, 2) == 0

        for q in range(4):
            parts = []
            for z in range(8):
                i = 8 * q + z
                f = xc[i]
                f = jnp.where(odd_x[:8], f, roll_l(f, 1))
                f = jnp.where(even_y[:8], f, pltpu.roll(f, 1, 0))
                parts.append(x0[i, :8] + x1[i, :8] + f)
            for c, f in enumerate(swap_blocks(parts, blk[:8])):
                send_back[4 * c + q] = f


        for k in FAR_FIRST:
            to = lax.rem(gz + k, SEGS)
            if k:
                back_copy(to).start()
            else:

                @pl.when(strip == gy)
                def _():
                    pltpu.make_async_copy(
                        send_back.at[gz], got_back.at[slot], back_recv.at[core]
                    ).start()

                @pl.when(strip != gy)
                def _():
                    back_copy(to).start()

        for q in range(4):
            for frm in (0, 1):

                @pl.when(core == frm)
                def _():
                    forward_copy(q, frm).wait_send()

    sent_all(1)


    column = lane[:8] // WIDE
    for to_core in (0, 1):
        rows = pl.ds(8 * to_core, 8)
        piece = got_back.at[pl.ds(to_core * TILES, TILES)]
        pltpu.make_async_copy(piece, piece, back_recv.at[to_core]).wait()
        for z in range(8):
            f = roll_l(got_back[to_core * TILES], -3 - 16 * z)
            for j in range(1, TILES):
                f = jnp.where(
                    column == j, roll_l(got_back[to_core * TILES + j], WIDE * j - 3 - 16 * z), f
                )
            o_ref[z, rows] = v_ref[z, rows] + f

    @pl.when(owner)
    def _():
        for k in range(SEGS):
            if k:
                back_copy(lax.rem(gz + k, SEGS)).wait_send()
            else:

                @pl.when(strip != gy)
                def _():
                    back_copy(gz).wait_send()


def body(electric_level, impurity_atoms, cell_materials):
    fields = (electric_level, impurity_atoms, cell_materials)
    line = pltpu.VMEM((32, 16, 128), F32)
    half = pltpu.VMEM((32, 8, 128), F32)
    vmem = pl.BlockSpec(memory_space=pltpu.VMEM)
    return pl.pallas_call(
        kernel,
        out_shape=jax.ShapeDtypeStruct(electric_level.shape, F32),
        in_specs=[pl.BlockSpec(memory_space=pltpu.HBM)] * 3,
        out_specs=vmem,
        scratch_shapes=[
            pltpu.VMEM(electric_level.shape, F32),
            pltpu.VMEM(electric_level.shape, jnp.int32),
            pltpu.VMEM(electric_level.shape, jnp.int32),
            pltpu.SemaphoreType.DMA((3,)),
            pltpu.VMEM((TILES, 3, 16, 128), F32),
            pltpu.VMEM((8, 4, 3, 16, 128), F32),
            pltpu.VMEM((SEGS, 8, 128), F32),
            pltpu.VMEM((OWNERS, 8, 128), F32),
            pltpu.VMEM((2, 33, 16, 128), F32),
        ]
        + [line] * 6
        + [half] * 2
        + [line] * 3
        + [half] * 3
        + [line] * 3
        + [half] * 3
        + [pltpu.SemaphoreType.DMA((2, 2, TILES))] * 2
        + [pltpu.SemaphoreType.DMA((TILES,)), pltpu.SemaphoreType.DMA((2, 4))]
        + [pltpu.SemaphoreType.DMA((4,))] * 2
        + [pltpu.SemaphoreType.DMA((SEGS,)), pltpu.SemaphoreType.DMA((2,))],
        compiler_params=pltpu.CompilerParams(
            collective_id=0, has_side_effects=True, vmem_limit_bytes=32 * 1024 * 1024
        ),
        cost_estimate=pl.CostEstimate(flops=20_000_000, bytes_accessed=262144, transcendentals=200_000),
        name="newton_step",
    )(*(pltpu.with_memory_space_constraint(f, pltpu.HBM) for f in fields))


def solution(mesh):
    placed = P("gz", "gy", None)
    return jax.shard_map(
        body, mesh=mesh, in_specs=(placed,) * 3, out_specs=placed, check_vma=False
    )
```
